128 devices in a mesh: clus: 128 (over x, z, y, core).
Axes of the slice: x: 4, y: 4, z: 4, core: 2. Of those that a mesh axis runs over, the one named last changes fastest.
Arguments:
- features: bfloat16 [262144, 128], P('clus'), may hold values from -6 to 6
- basis_t: bfloat16 [1024, 64, 256], P('clus'), may hold values from -0.375 to 0.375
- send_list: int32 [128, 128, 1], P('clus'), may hold values from 0 to 7
- couple_rows: int32 [49152], P('clus'), may hold values from 0 to 7
- couple_cols: int32 [49152], P('clus'), may hold values from 0 to 127, as said below
- couple_blocks: bfloat16 [49152, 4096], P('clus'), may hold values from -0.078125 to 0.078125
- near_rows: int32 [8192], P('clus'), may hold values from 0 to 7
- near_cols: int32 [8192], P('clus'), may hold values from 0 to 11
- near_blocks: bfloat16 [8192, 256, 256], P('clus'), may hold values from -0.09375 to 0.09375
Outputs:
- product: bfloat16 [262144, 128], P('clus')
The draws below stay inside these ranges and needn't reach their ends.
Inputs may be any that keep to these rules, and one draw needn't show every extreme that they name: Slot s of the slots that device p fills for device q holds local leaf send_list[p, q, s] of device p. `couple_cols`: on device d, slot p + s is the slot that device p fills for d with index s.
All inputs are finite; a program needn't handle non-finite values.
Results may differ from the reference program's by a relative error of at most 0.013.
Values may be sent and summed in bfloat16 or wider, within the bound.
A program may use at most 128 MiB of HBM per device.

```python
import jax
import jax.numpy as jnp
from jax import lax

LEAF = 256
RANK = 64
NRHS = 128
LPD = 8
HALO = 2
COUPLE_PER = 48
NEAR_PER = 8
LEAVES = 1024
ROWS = 262144
CB_DEV = 384
COUPLES = 49152
NB_DEV = 64
NEARS = 8192
SLOTS = 1
RECV = 128
N_CLUS = 128


def draw_couple_cols(key, part):
    key = jax.random.fold_in(key, 7)
    device_total = COUPLES // CB_DEV
    keys = jax.random.split(key, device_total)
    orders = jax.vmap(lambda one_key: jax.random.permutation(one_key, CB_DEV))(keys)
    return (orders % RECV).reshape(COUPLES).astype(jnp.int32)


def plant(values, own_key, smallest, largest):
    longest = values.shape.index(max(values.shape))
    spots = []
    for shift in (0, 1):
        where = [jax.random.randint(jax.random.fold_in(own_key, axis), (), 0, length) for axis, length in enumerate(values.shape)]
        where[longest] = (where[longest] + shift) % values.shape[longest]
        spots.append(tuple(where))
    return values.at[spots[0]].set(smallest).at[spots[1]].set(largest)


def shard_levels(key, dims, cuts, smallest, top_value):
    def one(dim, blocks):
        draws = jax.random.uniform(jax.random.fold_in(jax.random.fold_in(key, 6), dim), (blocks,), jnp.float32, smallest / len(cuts), top_value / len(cuts))
        return jnp.repeat(jnp.exp(draws), dims[dim] // blocks).reshape((-1,) + (1,) * (len(dims) - dim - 1))

    level = one(*cuts[0])
    for cut in cuts[1:]:
        level = level * one(*cut)
    return level


def gaussian(rng, shape, deviation, limit, cuts=(), held_as=jnp.bfloat16):
    gain = shard_levels(rng, shape, cuts, -0.22, 0.18) if cuts else 1.0
    values = jax.random.normal(rng, shape, jnp.float32) * deviation * gain
    return jnp.minimum(jnp.maximum(values, -limit), limit).astype(held_as)


def setup_inputs(seed: int = 0) -> dict:
    streams_of = jax.random.split(jax.random.key(seed), 10)
    features = gaussian(streams_of[0], (ROWS, NRHS), 1.0, 6.0, ((0, 128),))
    basis_t = gaussian(streams_of[1], (LEAVES, RANK, LEAF), LEAF ** -0.5, 0.375, ((0, 128),))
    send_list = plant(jax.random.randint(streams_of[2], (N_CLUS, N_CLUS, SLOTS), 0, LPD), jax.random.fold_in(streams_of[2], 1), 0, LPD - 1).astype(jnp.int32)
    couple_rows = plant(jax.random.randint(streams_of[3], (COUPLES,), 0, LPD), jax.random.fold_in(streams_of[3], 1), 0, LPD - 1).astype(jnp.int32)
    couple_cols = draw_couple_cols(jax.random.fold_in(streams_of[9], 71), 0)
    couple_blocks = gaussian(streams_of[5], (COUPLES, RANK * RANK), (RANK * 2 * COUPLE_PER) ** -0.5, 0.078125, ((0, 128),))
    near_rows = plant(jax.random.randint(streams_of[6], (NEARS,), 0, LPD), jax.random.fold_in(streams_of[6], 1), 0, LPD - 1).astype(jnp.int32)
    near_cols = plant(jax.random.randint(streams_of[7], (NEARS,), 0, LPD + 2 * HALO), jax.random.fold_in(streams_of[7], 1), 0, (LPD + 2 * HALO) - 1).astype(jnp.int32)
    near_blocks = gaussian(streams_of[8], (NEARS, LEAF, LEAF), (LEAF * 2 * NEAR_PER) ** -0.5, 0.09375, ((0, 128),))
    return dict(features=features, basis_t=basis_t, send_list=send_list, couple_rows=couple_rows, couple_cols=couple_cols, couple_blocks=couple_blocks, near_rows=near_rows, near_cols=near_cols, near_blocks=near_blocks)


def reference(features, basis_t, send_list, couple_rows, couple_cols, couple_blocks, near_rows, near_cols, near_blocks):
    local_x = features.reshape(LEAVES, LEAF, NRHS)
    coef = jnp.einsum("lrk,lkn->lrn", basis_t.astype(jnp.float32), local_x.astype(jnp.float32)).astype(jnp.bfloat16)
    owners = jnp.arange(COUPLES, dtype=jnp.int32) // CB_DEV
    sender = couple_cols // SLOTS
    within = couple_cols % SLOTS
    global_cols = sender * LPD + send_list[sender, owners, within]
    global_rows = owners * LPD + couple_rows
    blocks = couple_blocks.reshape(N_CLUS, CB_DEV, RANK, RANK)
    rows_split = global_rows.reshape(N_CLUS, CB_DEV)
    cols_split = global_cols.reshape(N_CLUS, CB_DEV)

    def far_step(total, item):
        block, row_ids, col_ids = item
        block_f = block.astype(jnp.float32)
        forward = jnp.einsum("kab,kbn->kan", block_f, coef[col_ids].astype(jnp.float32))
        mirror = jnp.einsum("kba,kbn->kan", block_f, coef[row_ids].astype(jnp.float32))
        total = total.at[row_ids].add(forward)
        total = total.at[col_ids].add(mirror)
        return total, None

    far, _ = lax.scan(far_step, jnp.zeros((LEAVES, RANK, NRHS), jnp.float32), (blocks, rows_split, cols_split))
    far = far.astype(jnp.bfloat16)
    down = jnp.einsum("lrk,lrn->lkn", basis_t.astype(jnp.float32), far.astype(jnp.float32))

    padded_x = jnp.pad(local_x, ((HALO, HALO), (0, 0), (0, 0)))
    near_owner = jnp.arange(NEARS, dtype=jnp.int32) // NB_DEV
    pad_rows = (near_owner * LPD + near_rows + HALO).reshape(N_CLUS, NB_DEV)
    pad_cols = (near_owner * LPD + near_cols).reshape(N_CLUS, NB_DEV)
    dense = near_blocks.reshape(N_CLUS, NB_DEV, LEAF, LEAF)

    def near_step(total, item):
        block, row_ids, col_ids = item
        block_f = block.astype(jnp.float32)
        forward = jnp.einsum("kij,kjn->kin", block_f, padded_x[col_ids].astype(jnp.float32))
        mirror = jnp.einsum("kji,kjn->kin", block_f, padded_x[row_ids].astype(jnp.float32))
        total = total.at[row_ids].add(forward)
        total = total.at[col_ids].add(mirror)
        return total, None

    near, _ = lax.scan(near_step, jnp.zeros((LEAVES + 2 * HALO, LEAF, NRHS), jnp.float32), (dense, pad_rows, pad_cols))
    result = down + near[HALO:HALO + LEAVES]
    return result.reshape(ROWS, NRHS).astype(jnp.bfloat16)
```

```python
import functools

import jax
import jax.numpy as jnp
from jax import lax
from jax.experimental import pallas as pl
from jax.experimental.pallas import tpu as pltpu
from jax.sharding import PartitionSpec as P

HALO = 2
MESH = pl.DeviceIdType.MESH
F32 = jnp.float32
BF16 = jnp.bfloat16


def chain(keys, count):
    n = keys.shape[0]
    at = jnp.arange(n, dtype=jnp.int32)
    same = (keys[:, None] == keys[None, :]) & (at[None, :] < at[:, None])
    prev = jnp.max(jnp.where(same, at[None, :], -1), axis=1)
    ids = jnp.arange(count, dtype=jnp.int32)
    last = jnp.max(jnp.where(ids[:, None] == keys[None, :], at[None, :], -1), axis=1)
    return jnp.where(prev < 0, n, prev), jnp.where(last < 0, n, last)


def kernel(
    n,
    leaves,
    rank,
    leaf,
    rhs,
    cb,
    nb,
    send_ref,
    cprev_ref,
    clast_ref,
    nrows_ref,
    ncols_ref,
    rprev_ref,
    rlast_ref,
    kprev_ref,
    klast_ref,
    qprev_ref,
    qlast_ref,
    x_hbm,
    basis_hbm,
    blocks_hbm,
    near_hbm,
    out_hbm,
    xext,
    basis,
    basis_t,
    blocks,
    near,
    coef,
    coef_f,
    coef_t,
    x_t,
    outgoing,
    received,
    plain,
    rolled,
    dense,
    sums,
    back,
    total,
    raw,
    chained,
    work,
    back_sum,
    near_sum,
    rim_out,
    rim_in,
    out,
    far_f,
    load_sem,
    send1,
    recv1,
    send2,
    recv2,
    hsend,
    hrecv,
    rsend,
    rrecv,
):
    me = lax.axis_index("clus")
    half = rank // 2
    lane = lax.broadcasted_iota(jnp.int32, (rank, 2 * rank), 1)
    low = lane < rank
    low_half = lax.broadcasted_iota(jnp.int32, (half, 2 * rank), 1) < rank

    barrier = pltpu.get_barrier_semaphore()

    load_x = pltpu.make_async_copy(x_hbm, xext.at[pl.ds(HALO, leaves)], load_sem.at[0])
    load_b = pltpu.make_async_copy(basis_hbm, basis, load_sem.at[1])
    load_s = pltpu.make_async_copy(blocks_hbm, blocks, load_sem.at[2])
    load_n = pltpu.make_async_copy(near_hbm, near, load_sem.at[3])
    load_x.start()
    load_b.start()
    load_s.start()
    load_n.start()

    def greet(i, carry):
        q = lax.rem(me + i, n)
        pl.semaphore_signal(barrier, inc=1, device_id=(q,), device_id_type=MESH)
        return carry

    lax.fori_loop(1, n, greet, 0)

    load_x.wait()
    load_b.wait()

    def coefficients(g, carry):
        c = jnp.dot(basis[g], xext[HALO + g], preferred_element_type=F32).astype(BF16)
        coef[g] = c
        coef_f[g] = c.astype(F32)
        return carry

    lax.fori_loop(0, leaves, coefficients, 0)

    pl.semaphore_wait(barrier, n - 1)

    def forward_copy(q):
        return pltpu.make_async_remote_copy(
            src_ref=outgoing.at[q],
            dst_ref=received.at[pl.ds(pl.multiple_of(me * rank, rank), rank)],
            send_sem=send1.at[q],
            recv_sem=recv1.at[me],
            device_id=(q,),
            device_id_type=MESH,
        )

    def send_coef(i, carry):
        q = lax.rem(me + i, n)
        outgoing[q] = coef[send_ref[q]]
        forward_copy(q).start()
        return carry

    lax.fori_loop(1, n, send_coef, 0)
    received[pl.ds(pl.multiple_of(me * rank, rank), rank), :] = coef[send_ref[me]]

    to_next = pltpu.make_async_remote_copy(
        src_ref=xext.at[pl.ds(leaves, HALO)],
        dst_ref=xext.at[pl.ds(0, HALO)],
        send_sem=hsend.at[0],
        recv_sem=hrecv.at[0],
        device_id=(lax.rem(me + 1, n),),
        device_id_type=MESH,
    )
    to_prior = pltpu.make_async_remote_copy(
        src_ref=xext.at[pl.ds(HALO, HALO)],
        dst_ref=xext.at[pl.ds(HALO + leaves, HALO)],
        send_sem=hsend.at[1],
        recv_sem=hrecv.at[1],
        device_id=(lax.rem(me + n - 1, n),),
        device_id_type=MESH,
    )
    has_next = me < n - 1
    has_prior = me > 0

    @pl.when(has_next)
    def _():
        to_next.start()

    @pl.when(has_prior)
    def _():
        to_prior.start()

    @pl.when(jnp.logical_not(has_prior))
    def _():
        xext[0:HALO] = jnp.zeros((HALO, leaf, rhs), BF16)

    @pl.when(jnp.logical_not(has_next))
    def _():
        xext[HALO + leaves :] = jnp.zeros((HALO, leaf, rhs), BF16)

    for pair in range(leaves // 2):
        rows = []
        for g in (2 * pair, 2 * pair + 1):
            for odd in range(2):
                rows.append(coef_f[g, pl.ds(odd, half, stride=2), :])
        tile = jnp.concatenate(rows, axis=0)
        coef_t[:, pair * 2 * rank : (pair + 1) * 2 * rank] = tile.T.astype(BF16)

    load_s.wait()

    chained[cb] = jnp.zeros((half, 2 * rank), F32)
    plain[cb] = jnp.zeros((half, 2 * rank), BF16)
    rolled[cb] = jnp.zeros((half, 2 * rank), BF16)

    def spread(t, carry):
        for j in range(half):
            piece = blocks[pl.ds(pl.multiple_of(t * 16, 16), 16), j * 2 * rank : (j + 1) * 2 * rank]
            raw[pl.ds(j, 16, stride=half), :] = piece.astype(F32)
        for s in range(16):
            k = t * 16 + s
            value = raw[s * half : (s + 1) * half, :] + chained[cprev_ref[k]]
            chained[k] = value
            plain[k] = value.astype(BF16)
            rolled[k] = pltpu.roll(value, rank, 1).astype(BF16)
        return carry

    lax.fori_loop(0, cb // 16, spread, 0)

    groups = n // 4
    my_group = me // 4

    def back_copy(q):
        return pltpu.make_async_remote_copy(
            src_ref=sums.at[q],
            dst_ref=back.at[me],
            send_sem=send2.at[q],
            recv_sem=recv2.at[me],
            device_id=(q,),
            device_id_type=MESH,
        )

    def mirror(i, carry):
        g = lax.rem(my_group + i, groups)
        for pair in range(2):
            for r in range(leaves):
                k0 = clast_ref[(g * 4 + 2 * pair) * leaves + r]
                k1 = clast_ref[(g * 4 + 2 * pair + 1) * leaves + r]
                upper = jnp.where(low_half, plain[k0], rolled[k1])
                lower = jnp.where(low_half, rolled[k0], plain[k1])
                cols = pl.ds(pair * 2 * rank, 2 * rank)
                dense[g, r * rank : r * rank + half, cols] = upper
                dense[g, r * rank + half : (r + 1) * rank, cols] = lower
        product = jnp.dot(coef_t[...], dense[g], preferred_element_type=F32)
        for pair in range(2):
            part = product[:, pair * 2 * rank : (pair + 1) * 2 * rank]
            top, bottom = part[:rank], part[rank:]
            turned = pltpu.roll(jnp.where(low, bottom, top), rank, 1)
            sums[g * 4 + 2 * pair] = jnp.where(low, top, turned).astype(BF16)
            sums[g * 4 + 2 * pair + 1] = jnp.where(low, turned, bottom).astype(BF16)
        for s in range(4):
            q = g * 4 + s

            @pl.when(q != me)
            def _():
                back_copy(q).start()

            @pl.when(q == me)
            def _():
                back[me] = sums[me]

        return carry

    lax.fori_loop(0, groups, mirror, 0)

    for g in range(leaves):
        x_t[g] = xext[HALO + g].astype(F32).T.astype(BF16)
        basis_t[g] = basis[g].astype(F32).T.astype(BF16)

    @pl.when(has_prior)
    def _():
        to_next.wait_recv()

    @pl.when(has_next)
    def _():
        to_prior.wait_recv()

    load_n.wait()
    work[nb] = jnp.zeros((leaf, rhs), F32)

    def near_rows(k, carry):
        y = jnp.dot(near[k], xext[ncols_ref[k]], preferred_element_type=F32)
        work[k] = y + work[rprev_ref[k]]
        return carry

    lax.fori_loop(0, nb, near_rows, 0)
    for g in range(leaves):
        near_sum[g] = work[rlast_ref[g]]

    def near_cols(k, carry):
        y = jnp.dot(x_t[nrows_ref[k]], near[k], preferred_element_type=F32)
        before = work[kprev_ref[k]]
        for h in range(2):
            rows = slice(h * rhs, (h + 1) * rhs)
            work[k, rows, :] = y[:, rows] + before[rows]
        return carry

    lax.fori_loop(0, nb, near_cols, 0)

    def spread_of(c):
        return work[klast_ref[c]]

    for h in range(HALO):
        rim_out[0, h] = spread_of(h).astype(BF16)
        rim_out[1, h] = spread_of(HALO + leaves + h).astype(BF16)
    rim_prior = pltpu.make_async_remote_copy(
        src_ref=rim_out.at[0],
        dst_ref=rim_in.at[0],
        send_sem=rsend.at[0],
        recv_sem=rrecv.at[0],
        device_id=(lax.rem(me + n - 1, n),),
        device_id_type=MESH,
    )
    rim_next = pltpu.make_async_remote_copy(
        src_ref=rim_out.at[1],
        dst_ref=rim_in.at[1],
        send_sem=rsend.at[1],
        recv_sem=rrecv.at[1],
        device_id=(lax.rem(me + 1, n),),
        device_id_type=MESH,
    )

    @pl.when(has_prior)
    def _():
        rim_prior.start()

    @pl.when(has_next)
    def _():
        rim_next.start()

    def add_turned(g, y):
        for h in range(2):
            rows = slice(h * rhs, (h + 1) * rhs)
            near_sum[g, rows, :] += y[rows].T

    for g in range(leaves):
        add_turned(g, spread_of(HALO + g))

    total[...] = jnp.zeros_like(total)
    step = min(4, groups)

    def forward(i, carry):
        for s in range(4 * step):
            q = i * 4 * step + s

            @pl.when(q != me)
            def _():
                pltpu.make_async_remote_copy(
                    src_ref=outgoing.at[q],
                    dst_ref=received.at[pl.ds(pl.multiple_of(q * rank, rank), rank)],
                    send_sem=send1.at[q],
                    recv_sem=recv1.at[q],
                    device_id=(q,),
                    device_id_type=MESH,
                ).wait_recv()

        acc = total[...]
        for s in range(step):
            g = i * step + s
            c = received[pl.ds(pl.multiple_of(g * 4 * rank, 4 * rank), 4 * rank), :]
            acc = acc + jnp.dot(dense[g], c, preferred_element_type=F32)
        total[...] = acc
        return carry

    lax.fori_loop(0, groups // step, forward, 0)

    @pl.when(has_next)
    def _():
        rim_prior.wait_recv()
        for h in range(HALO):
            add_turned(leaves - HALO + h, rim_in[0, h].astype(F32))

    @pl.when(has_prior)
    def _():
        rim_next.wait_recv()
        for h in range(HALO):
            add_turned(h, rim_in[1, h].astype(F32))

    back_sum[n] = jnp.zeros((rank, rhs), F32)

    def returned(q, carry):
        @pl.when(q != me)
        def _():
            pltpu.make_async_remote_copy(
                src_ref=sums.at[q],
                dst_ref=back.at[q],
                send_sem=send2.at[q],
                recv_sem=recv2.at[q],
                device_id=(q,),
                device_id_type=MESH,
            ).wait_recv()

        back_sum[q] = back[q].astype(F32) + back_sum[qprev_ref[q]]
        return carry

    lax.fori_loop(0, n, returned, 0)

    for g in range(leaves):
        y = back_sum[qlast_ref[g]]
        turned = jnp.concatenate([y, pltpu.roll(y, rank, 1)], axis=0).T
        far_f[g, pl.ds(0, half, stride=2), :] = total[g * rank : g * rank + half, :]
        far_f[g, pl.ds(1, half, stride=2), :] = total[g * rank + half : (g + 1) * rank, :]
        far = (far_f[g] + turned[:rank]).astype(BF16)
        down = jnp.dot(basis_t[g], far, preferred_element_type=F32)
        out[g * leaf : (g + 1) * leaf, :] = (down + near_sum[g]).astype(BF16)

    store = pltpu.make_async_copy(out, out_hbm, load_sem.at[0])
    store.start()

    def drain(i, carry):
        q = lax.rem(me + i, n)
        forward_copy(q).wait_send()
        back_copy(q).wait_send()
        return carry

    lax.fori_loop(1, n, drain, 0)

    @pl.when(has_next)
    def _():
        to_next.wait_send()
        rim_next.wait_send()

    @pl.when(has_prior)
    def _():
        to_prior.wait_send()
        rim_prior.wait_send()

    store.wait()


def per_device(
    features,
    basis_t,
    send_list,
    couple_rows,
    couple_cols,
    couple_blocks,
    near_rows,
    near_cols,
    near_blocks,
):
    n = lax.axis_size("clus")
    leaves, rank, leaf = basis_t.shape
    rhs = features.shape[1]
    cb, nb = couple_blocks.shape[0], near_blocks.shape[0]
    send = send_list.reshape(-1)
    cprev, clast = chain(couple_cols * leaves + couple_rows, n * leaves)
    rprev, rlast = chain(near_rows, leaves)
    kprev, klast = chain(near_cols, leaves + 2 * HALO)
    qprev, qlast = chain(send, leaves)
    half = rank // 2
    wide = leaves + 2 * HALO
    dma = pltpu.SemaphoreType.DMA
    smem = pl.BlockSpec(memory_space=pltpu.SMEM)
    anywhere = pl.BlockSpec(memory_space=pl.ANY)
    return pl.pallas_call(
        functools.partial(kernel, n, leaves, rank, leaf, rhs, cb, nb),
        out_shape=jax.ShapeDtypeStruct(features.shape, BF16),
        in_specs=[smem] * 11 + [anywhere] * 4,
        out_specs=anywhere,
        scratch_shapes=[
            pltpu.VMEM((wide, leaf, rhs), BF16),
            pltpu.VMEM((leaves, rank, leaf), BF16),
            pltpu.VMEM((leaves, leaf, rank), BF16),
            pltpu.VMEM(couple_blocks.shape, BF16),
            pltpu.VMEM(near_blocks.shape, BF16),
            pltpu.VMEM((leaves, rank, rhs), BF16),
            pltpu.VMEM((leaves, rank, rhs), F32),
            pltpu.VMEM((rhs, leaves * rank), BF16),
            pltpu.VMEM((leaves, rhs, leaf), BF16),
            pltpu.VMEM((n, rank, rhs), BF16),
            pltpu.VMEM((n * rank, rhs), BF16),
            pltpu.VMEM((cb + 1, half, 2 * rank), BF16),
            pltpu.VMEM((cb + 1, half, 2 * rank), BF16),
            pltpu.VMEM((n // 4, leaves * rank, 4 * rank), BF16),
            pltpu.VMEM((n, rank, rhs), BF16),
            pltpu.VMEM((n, rank, rhs), BF16),
            pltpu.VMEM((leaves * rank, rhs), F32),
            pltpu.VMEM((16 * half, 2 * rank), F32),
            pltpu.VMEM((cb + 1, half, 2 * rank), F32),
            pltpu.VMEM((nb + 1, leaf, rhs), F32),
            pltpu.VMEM((n + 1, rank, rhs), F32),
            pltpu.VMEM((leaves, leaf, rhs), F32),
            pltpu.VMEM((2, HALO, leaf, rhs), BF16),
            pltpu.VMEM((2, HALO, leaf, rhs), BF16),
            pltpu.VMEM((leaves * leaf, rhs), BF16),
            pltpu.VMEM((leaves, rank, rhs), F32),
            dma((4,)),
            dma((n,)),
            dma((n,)),
            dma((n,)),
            dma((n,)),
            dma((2,)),
            dma((2,)),
            dma((2,)),
            dma((2,)),
        ],
        compiler_params=pltpu.CompilerParams(
            collective_id=0, has_side_effects=True, vmem_limit_bytes=60 * 1024 * 1024
        ),
    )(
        send,
        cprev,
        clast,
        near_rows,
        near_cols,
        rprev,
        rlast,
        kprev,
        klast,
        qprev,
        qlast,
        features.reshape(leaves, leaf, rhs),
        basis_t,
        couple_blocks,
        near_blocks,
    )


def solution(mesh):
    placed = (
        P("clus", None),
        P("clus", None, None),
        P("clus", None, None),
        P("clus"),
        P("clus"),
        P("clus", None),
        P("clus"),
        P("clus"),
        P("clus", None, None),
    )
    return jax.shard_map(
        per_device, mesh=mesh, in_specs=placed, out_specs=P("clus", None), check_vma=False
    )
```

```python
import functools
import random

import jax
import jax.numpy as jnp
import numpy as np
from jax import lax
from jax.experimental import pallas as pl
from jax.experimental.pallas import tpu as pltpu
from jax.sharding import PartitionSpec as P

HALO = 2
MESH = pl.DeviceIdType.MESH
F32 = jnp.float32
BF16 = jnp.bfloat16


def chains(parts):
    keys, first, size = [], [], []
    seen, length = 0, 0
    for part, count in parts:
        keys.append(part + seen)
        first.append(np.stack([np.full(part.shape[0], length), np.full(part.shape[0], part.shape[0])]))
        size.append(np.stack([np.full(count, length), np.full(count, part.shape[0])]))
        seen, length = seen + count, length + part.shape[0]
    keys = jnp.concatenate(keys)
    at = jnp.arange(length, dtype=jnp.int32)
    ids = jnp.arange(seen, dtype=jnp.int32)
    same = (keys[:, None] == keys[None, :]) & (at[None, :] < at[:, None])
    prev = jnp.max(jnp.where(same, at[None, :], -1), axis=1)
    last = jnp.max(jnp.where(ids[:, None] == keys[None, :], at[None, :], -1), axis=1)
    first, size = (np.concatenate(v, axis=1).astype(np.int32) for v in (first, size))
    prev = jnp.where(prev < 0, first[1], prev - first[0])
    last = jnp.where(last < 0, size[1], last - size[0])
    return prev, last


def far_first(n):
    steps = [(o // 32, o // 8 % 4, o // 2 % 4, o % 2) for o in range(1, n)]
    random.Random(0).shuffle(steps)
    steps.sort(key=lambda o: -sum(min(v, 4 - v) for v in o[:3]))
    return steps


def kernel(
    n,
    leaves,
    rank,
    leaf,
    rhs,
    cb,
    nb,
    send_ref,
    nrows_ref,
    ncols_ref,
    prev_ref,
    last_ref,
    x_hbm,
    basis_hbm,
    blocks_hbm,
    near_hbm,
    out_hbm,
    xext,
    basis,
    basis_t,
    blocks,
    near,
    coef,
    coef_f,
    coef_t,
    x_t,
    outgoing,
    received,
    plain,
    rolled,
    dense,
    sums,
    back,
    total,
    raw,
    chained,
    work,
    back_sum,
    near_sum,
    rim_out,
    rim_in,
    out,
    far_f,
    load_sem,
    send1,
    recv1,
    send2,
    recv2,
    hsend,
    hrecv,
    rsend,
    rrecv,
):
    me = lax.axis_index("clus")
    cprev, rprev, kprev, qprev = 0, cb, cb + nb, cb + 2 * nb
    clast, rlast = 0, n * leaves
    klast, qlast = rlast + leaves, rlast + 2 * leaves + 2 * HALO
    half = rank // 2
    lane = lax.broadcasted_iota(jnp.int32, (rank, 2 * rank), 1)
    low = lane < rank
    low_half = lax.broadcasted_iota(jnp.int32, (half, 2 * rank), 1) < rank

    barrier = pltpu.get_barrier_semaphore()

    load_x = pltpu.make_async_copy(x_hbm, xext.at[pl.ds(HALO, leaves)], load_sem.at[0])
    load_b = pltpu.make_async_copy(basis_hbm, basis, load_sem.at[1])
    load_s = pltpu.make_async_copy(blocks_hbm, blocks, load_sem.at[2])
    load_n = pltpu.make_async_copy(near_hbm, near, load_sem.at[3])
    load_x.start()
    load_b.start()
    load_s.start()
    load_n.start()

    def greet(i, carry):
        q = lax.rem(me + i, n)
        pl.semaphore_signal(barrier, inc=1, device_id=(q,), device_id_type=MESH)
        return carry

    lax.fori_loop(1, n, greet, 0)

    load_x.wait()
    load_b.wait()

    def coefficients(g, carry):
        c = jnp.dot(basis[g], xext[HALO + g], preferred_element_type=F32).astype(BF16)
        coef[g] = c
        coef_f[g] = c.astype(F32)
        return carry

    lax.fori_loop(0, leaves, coefficients, 0)

    pl.semaphore_wait(barrier, n - 1)

    def forward_copy(q):
        return pltpu.make_async_remote_copy(
            src_ref=outgoing.at[q],
            dst_ref=received.at[pl.ds(pl.multiple_of(me * rank, rank), rank)],
            send_sem=send1.at[q],
            recv_sem=recv1.at[me],
            device_id=(q,),
            device_id_type=MESH,
        )

    def peer(step):
        x, z, y, core = me // 32, me // 8 % 4, me // 2 % 4, me % 2
        dx, dz, dy, dc = step
        return (((x + dx) % (n // 32) * 4 + (z + dz) % 4) * 4 + (y + dy) % 4) * 2 + (core + dc) % 2

    for step in far_first(n):
        q = peer(step)
        outgoing[q] = coef[send_ref[q]]
        forward_copy(q).start()
    received[pl.ds(pl.multiple_of(me * rank, rank), rank), :] = coef[send_ref[me]]

    to_next = pltpu.make_async_remote_copy(
        src_ref=xext.at[pl.ds(leaves, HALO)],
        dst_ref=xext.at[pl.ds(0, HALO)],
        send_sem=hsend.at[0],
        recv_sem=hrecv.at[0],
        device_id=(lax.rem(me + 1, n),),
        device_id_type=MESH,
    )
    to_prior = pltpu.make_async_remote_copy(
        src_ref=xext.at[pl.ds(HALO, HALO)],
        dst_ref=xext.at[pl.ds(HALO + leaves, HALO)],
        send_sem=hsend.at[1],
        recv_sem=hrecv.at[1],
        device_id=(lax.rem(me + n - 1, n),),
        device_id_type=MESH,
    )
    has_next = me < n - 1
    has_prior = me > 0

    @pl.when(has_next)
    def _():
        to_next.start()

    @pl.when(has_prior)
    def _():
        to_prior.start()

    @pl.when(jnp.logical_not(has_prior))
    def _():
        xext[0:HALO] = jnp.zeros((HALO, leaf, rhs), BF16)

    @pl.when(jnp.logical_not(has_next))
    def _():
        xext[HALO + leaves :] = jnp.zeros((HALO, leaf, rhs), BF16)

    for pair in range(leaves // 2):
        rows = []
        for g in (2 * pair, 2 * pair + 1):
            for odd in range(2):
                rows.append(coef_f[g, pl.ds(odd, half, stride=2), :])
        tile = jnp.concatenate(rows, axis=0)
        coef_t[:, pair * 2 * rank : (pair + 1) * 2 * rank] = tile.T.astype(BF16)

    load_s.wait()

    chained[cb] = jnp.zeros((half, 2 * rank), F32)
    plain[cb] = jnp.zeros((half, 2 * rank), BF16)
    rolled[cb] = jnp.zeros((half, 2 * rank), BF16)

    def spread(t, carry):
        for j in range(half):
            piece = blocks[pl.ds(pl.multiple_of(t * 16, 16), 16), j * 2 * rank : (j + 1) * 2 * rank]
            raw[pl.ds(j, 16, stride=half), :] = piece.astype(F32)
        for s in range(16):
            k = t * 16 + s
            value = raw[s * half : (s + 1) * half, :] + chained[prev_ref[cprev + k]]
            chained[k] = value
            plain[k] = value.astype(BF16)
            rolled[k] = pltpu.roll(value, rank, 1).astype(BF16)
        return carry

    lax.fori_loop(0, cb // 16, spread, 0, unroll=1)

    groups = n // 4
    my_group = me // 4

    def back_copy(q):
        return pltpu.make_async_remote_copy(
            src_ref=sums.at[q],
            dst_ref=back.at[me],
            send_sem=send2.at[q],
            recv_sem=recv2.at[me],
            device_id=(q,),
            device_id_type=MESH,
        )

    def mirror(i, carry):
        g = lax.rem(my_group + i * 13, groups)
        rows = []
        for r in range(leaves):
            upper, lower = [], []
            for pair in range(2):
                k0 = last_ref[clast + (g * 4 + 2 * pair) * leaves + r]
                k1 = last_ref[clast + (g * 4 + 2 * pair + 1) * leaves + r]
                upper.append(jnp.where(low_half, plain[k0], rolled[k1]))
                lower.append(jnp.where(low_half, rolled[k0], plain[k1]))
            rows.append(jnp.concatenate(upper, axis=1))
            rows.append(jnp.concatenate(lower, axis=1))
        tile = jnp.concatenate(rows, axis=0)
        dense[g] = tile
        product = jnp.dot(coef_t[...], tile, preferred_element_type=F32)
        for pair in range(2):
            part = product[:, pair * 2 * rank : (pair + 1) * 2 * rank]
            top, bottom = part[:rank], part[rank:]
            turned = pltpu.roll(jnp.where(low, bottom, top), rank, 1)
            sums[g * 4 + 2 * pair] = jnp.where(low, top, turned).astype(BF16)
            sums[g * 4 + 2 * pair + 1] = jnp.where(low, turned, bottom).astype(BF16)
        for s in range(4):
            q = g * 4 + s

            @pl.when(q != me)
            def _():
                back_copy(q).start()

            @pl.when(q == me)
            def _():
                back[me] = sums[me]

        return carry

    lax.fori_loop(0, groups, mirror, 0, unroll=2)

    for g in range(leaves):
        x_t[g] = xext[HALO + g].astype(F32).T.astype(BF16)
        basis_t[g] = basis[g].astype(F32).T.astype(BF16)

    @pl.when(has_prior)
    def _():
        to_next.wait_recv()

    @pl.when(has_next)
    def _():
        to_prior.wait_recv()

    load_n.wait()
    work[nb] = jnp.zeros((leaf, rhs), F32)

    def near_rows(k, carry):
        y = jnp.dot(near[k], xext[ncols_ref[k]], preferred_element_type=F32)
        work[k] = y + work[prev_ref[rprev + k]]
        return carry

    lax.fori_loop(0, nb, near_rows, 0, unroll=8)
    for g in range(leaves):
        near_sum[g] = work[last_ref[rlast + g]]

    def near_cols(k, carry):
        y = jnp.dot(x_t[nrows_ref[k]], near[k], preferred_element_type=F32)
        before = work[prev_ref[kprev + k]]
        for h in range(2):
            rows = slice(h * rhs, (h + 1) * rhs)
            work[k, rows, :] = y[:, rows] + before[rows]
        return carry

    lax.fori_loop(0, nb, near_cols, 0, unroll=8)

    def spread_of(c):
        return work[last_ref[klast + c]]

    for h in range(HALO):
        rim_out[0, h] = spread_of(h).astype(BF16)
        rim_out[1, h] = spread_of(HALO + leaves + h).astype(BF16)
    rim_prior = pltpu.make_async_remote_copy(
        src_ref=rim_out.at[0],
        dst_ref=rim_in.at[0],
        send_sem=rsend.at[0],
        recv_sem=rrecv.at[0],
        device_id=(lax.rem(me + n - 1, n),),
        device_id_type=MESH,
    )
    rim_next = pltpu.make_async_remote_copy(
        src_ref=rim_out.at[1],
        dst_ref=rim_in.at[1],
        send_sem=rsend.at[1],
        recv_sem=rrecv.at[1],
        device_id=(lax.rem(me + 1, n),),
        device_id_type=MESH,
    )

    @pl.when(has_prior)
    def _():
        rim_prior.start()

    @pl.when(has_next)
    def _():
        rim_next.start()

    def add_turned(g, y):
        for h in range(2):
            rows = slice(h * rhs, (h + 1) * rhs)
            near_sum[g, rows, :] += y[rows].T

    for g in range(leaves):
        add_turned(g, spread_of(HALO + g))

    total[...] = jnp.zeros_like(total)
    step = min(4, groups)

    def forward(i, carry):
        for s in range(4 * step):
            q = i * 4 * step + s

            @pl.when(q != me)
            def _():
                pltpu.make_async_remote_copy(
                    src_ref=outgoing.at[q],
                    dst_ref=received.at[pl.ds(pl.multiple_of(q * rank, rank), rank)],
                    send_sem=send1.at[q],
                    recv_sem=recv1.at[q],
                    device_id=(q,),
                    device_id_type=MESH,
                ).wait_recv()

        acc = total[...]
        for s in range(step):
            g = i * step + s
            c = received[pl.ds(pl.multiple_of(g * 4 * rank, 4 * rank), 4 * rank), :]
            acc = acc + jnp.dot(dense[g], c, preferred_element_type=F32)
        total[...] = acc
        return carry

    lax.fori_loop(0, groups // step, forward, 0)

    @pl.when(has_next)
    def _():
        rim_prior.wait_recv()
        for h in range(HALO):
            add_turned(leaves - HALO + h, rim_in[0, h].astype(F32))

    @pl.when(has_prior)
    def _():
        rim_next.wait_recv()
        for h in range(HALO):
            add_turned(h, rim_in[1, h].astype(F32))

    back_sum[n] = jnp.zeros((rank, rhs), F32)

    def returned(q, carry):
        @pl.when(q != me)
        def _():
            pltpu.make_async_remote_copy(
                src_ref=sums.at[q],
                dst_ref=back.at[q],
                send_sem=send2.at[q],
                recv_sem=recv2.at[q],
                device_id=(q,),
                device_id_type=MESH,
            ).wait_recv()

        back_sum[q] = back[q].astype(F32) + back_sum[prev_ref[qprev + q]]
        return carry

    lax.fori_loop(0, n, returned, 0, unroll=4)

    for g in range(leaves):
        y = back_sum[last_ref[qlast + g]]
        turned = jnp.concatenate([y, pltpu.roll(y, rank, 1)], axis=0).T
        far_f[g, pl.ds(0, half, stride=2), :] = total[g * rank : g * rank + half, :]
        far_f[g, pl.ds(1, half, stride=2), :] = total[g * rank + half : (g + 1) * rank, :]
        far = (far_f[g] + turned[:rank]).astype(BF16)
        down = jnp.dot(basis_t[g], far, preferred_element_type=F32)
        out[g * leaf : (g + 1) * leaf, :] = (down + near_sum[g]).astype(BF16)

    store = pltpu.make_async_copy(out, out_hbm, load_sem.at[0])
    store.start()

    def drain(i, carry):
        q = lax.rem(me + i, n)
        forward_copy(q).wait_send()
        back_copy(q).wait_send()
        return carry

    lax.fori_loop(1, n, drain, 0)

    @pl.when(has_next)
    def _():
        to_next.wait_send()
        rim_next.wait_send()

    @pl.when(has_prior)
    def _():
        to_prior.wait_send()
        rim_prior.wait_send()

    store.wait()


def per_device(
    features,
    basis_t,
    send_list,
    couple_rows,
    couple_cols,
    couple_blocks,
    near_rows,
    near_cols,
    near_blocks,
):
    n = lax.axis_size("clus")
    leaves, rank, leaf = basis_t.shape
    rhs = features.shape[1]
    cb, nb = couple_blocks.shape[0], near_blocks.shape[0]
    send = send_list.reshape(-1)
    prev, last = chains(
        [
            (couple_cols * leaves + couple_rows, n * leaves),
            (near_rows, leaves),
            (near_cols, leaves + 2 * HALO),
            (send, leaves),
        ]
    )
    half = rank // 2
    wide = leaves + 2 * HALO
    dma = pltpu.SemaphoreType.DMA
    smem = pl.BlockSpec(memory_space=pltpu.SMEM)
    anywhere = pl.BlockSpec(memory_space=pl.ANY)
    return pl.pallas_call(
        functools.partial(kernel, n, leaves, rank, leaf, rhs, cb, nb),
        out_shape=jax.ShapeDtypeStruct(features.shape, BF16),
        in_specs=[smem] * 5 + [anywhere] * 4,
        out_specs=anywhere,
        scratch_shapes=[
            pltpu.VMEM((wide, leaf, rhs), BF16),
            pltpu.VMEM((leaves, rank, leaf), BF16),
            pltpu.VMEM((leaves, leaf, rank), BF16),
            pltpu.VMEM(couple_blocks.shape, BF16),
            pltpu.VMEM(near_blocks.shape, BF16),
            pltpu.VMEM((leaves, rank, rhs), BF16),
            pltpu.VMEM((leaves, rank, rhs), F32),
            pltpu.VMEM((rhs, leaves * rank), BF16),
            pltpu.VMEM((leaves, rhs, leaf), BF16),
            pltpu.VMEM((n, rank, rhs), BF16),
            pltpu.VMEM((n * rank, rhs), BF16),
            pltpu.VMEM((cb + 1, half, 2 * rank), BF16),
            pltpu.VMEM((cb + 1, half, 2 * rank), BF16),
            pltpu.VMEM((n // 4, leaves * rank, 4 * rank), BF16),
            pltpu.VMEM((n, rank, rhs), BF16),
            pltpu.VMEM((n, rank, rhs), BF16),
            pltpu.VMEM((leaves * rank, rhs), F32),
            pltpu.VMEM((16 * half, 2 * rank), F32),
            pltpu.VMEM((cb + 1, half, 2 * rank), F32),
            pltpu.VMEM((nb + 1, leaf, rhs), F32),
            pltpu.VMEM((n + 1, rank, rhs), F32),
            pltpu.VMEM((leaves, leaf, rhs), F32),
            pltpu.VMEM((2, HALO, leaf, rhs), BF16),
            pltpu.VMEM((2, HALO, leaf, rhs), BF16),
            pltpu.VMEM((leaves * leaf, rhs), BF16),
            pltpu.VMEM((leaves, rank, rhs), F32),
            dma((4,)),
            dma((n,)),
            dma((n,)),
            dma((n,)),
            dma((n,)),
            dma((2,)),
            dma((2,)),
            dma((2,)),
            dma((2,)),
        ],
        compiler_params=pltpu.CompilerParams(
            collective_id=0, has_side_effects=True, vmem_limit_bytes=60 * 1024 * 1024
        ),
    )(
        send,
        near_rows,
        near_cols,
        prev,
        last,
        features.reshape(leaves, leaf, rhs),
        basis_t,
        couple_blocks,
        near_blocks,
    )


def solution(mesh):
    placed = (
        P("clus", None),
        P("clus", None, None),
        P("clus", None, None),
        P("clus"),
        P("clus"),
        P("clus", None),
        P("clus"),
        P("clus"),
        P("clus", None, None),
    )
    return jax.shard_map(
        per_device, mesh=mesh, in_specs=placed, out_specs=P("clus", None), check_vma=False
    )
```

```python
import functools
import random

import jax
import jax.numpy as jnp
from jax import lax
from jax.experimental import pallas as pl
from jax.experimental.pallas import tpu as pltpu
from jax.sharding import PartitionSpec as P

HALO = 2
MESH = pl.DeviceIdType.MESH
F32 = jnp.float32
BF16 = jnp.bfloat16


def chains(keys_ref, prev_ref, last_ref, parts, id_parts):
    blocks = keys_ref.shape[0]
    row = lax.broadcasted_iota(jnp.int32, (128, 128), 0)
    col = lax.broadcasted_iota(jnp.int32, (128, 128), 1)
    down = [jnp.broadcast_to(keys_ref[b : b + 1, :], (128, 128)).T for b in range(blocks)]
    lane = lax.broadcasted_iota(jnp.int32, (1, 128), 1)

    def settle(found, place, bounds):
        start, length = jnp.zeros_like(place), jnp.zeros_like(place)
        for first, (at, size) in bounds:
            start = jnp.where(place >= first, at, start)
            length = jnp.where(place >= first, size, length)
        return jnp.where(found < 0, length, jnp.clip(found - start, 0, length))

    for b in range(blocks):
        key = keys_ref[b : b + 1, :]
        best = jnp.full((128, 128), -1, jnp.int32)
        for other in range(b + 1):
            hit = down[other] == key
            if other == b:
                hit = hit & (row < col)
            best = jnp.where(hit, row + other * 128, best)
        found = jnp.max(best, axis=0, keepdims=True)
        prev_ref[b : b + 1, :] = settle(found, lane + b * 128, [(start, (start, size)) for start, size in parts])
    for b in range(last_ref.shape[0]):
        best = jnp.full((128, 128), -1, jnp.int32)
        for other in range(blocks):
            best = jnp.where(down[other] == lane + b * 128, row + other * 128, best)
        found = jnp.max(best, axis=0, keepdims=True)
        last_ref[b : b + 1, :] = settle(found, lane + b * 128, [(first, parts[part]) for first, part in id_parts])


def near_first(n):
    steps = [(o // 32, o // 8 % 4, o // 2 % 4, o % 2) for o in range(1, n)]
    random.Random(0).shuffle(steps)
    steps.sort(key=lambda o: sum(min(v, 4 - v) for v in o[:3]))
    return steps


def kernel(
    n,
    leaves,
    rank,
    leaf,
    rhs,
    cb,
    nb,
    key_ref,
    keys,
    x_hbm,
    basis_hbm,
    blocks_hbm,
    near_hbm,
    out_hbm,
    xext,
    basis,
    basis_t,
    blocks,
    near,
    coef,
    coef_f,
    coef_t,
    x_t,
    outgoing,
    received,
    plain,
    rolled,
    dense,
    sums,
    back,
    total,
    raw,
    chained,
    work,
    back_sum,
    near_sum,
    rim_out,
    rim_in,
    out,
    far_f,
    prev_v,
    last_v,
    prev_s,
    last_s,
    load_sem,
    send1,
    recv1,
    send2,
    recv2,
    hsend,
    hrecv,
    rsend,
    rrecv,
):
    me = lax.axis_index("clus")
    base = last_v.shape[0] * 128 - 128
    rprev, kprev, qprev = cb, cb + nb, cb + 2 * nb
    rlast, klast, qlast = base, base + leaves, base + 2 * leaves + 2 * HALO
    parts = [(0, cb), (rprev, nb), (kprev, nb), (qprev, n)]
    id_parts = [(0, 0), (rlast, 1), (klast, 2), (qlast, 3)]

    def at(ref, i):
        return ref[i // 128, i % 128]

    def target(q):
        return jnp.maximum(at(key_ref, qprev + q) - qlast, 0)

    half = rank // 2
    lane = lax.broadcasted_iota(jnp.int32, (rank, 2 * rank), 1)
    low = lane < rank
    low_half = lax.broadcasted_iota(jnp.int32, (half, 2 * rank), 1) < rank

    barrier = pltpu.get_barrier_semaphore()

    load_x = pltpu.make_async_copy(x_hbm, xext.at[pl.ds(HALO, leaves)], load_sem.at[0])
    load_b = pltpu.make_async_copy(basis_hbm, basis, load_sem.at[1])
    load_s = pltpu.make_async_copy(blocks_hbm, blocks, load_sem.at[2])
    load_n = pltpu.make_async_copy(near_hbm, near, load_sem.at[3])
    load_x.start()
    load_b.start()
    load_s.start()

    def greet(i, carry):
        q = lax.rem(me + i, n)
        pl.semaphore_signal(barrier, inc=1, device_id=(q,), device_id_type=MESH)
        return carry

    lax.fori_loop(1, n, greet, 0)

    load_x.wait()
    load_b.wait()

    def coefficients(g, carry):
        c = jnp.dot(basis[g], xext[HALO + g], preferred_element_type=F32).astype(BF16)
        coef[g] = c
        coef_f[g] = c.astype(F32)
        return carry

    lax.fori_loop(0, leaves, coefficients, 0, unroll=leaves)
    load_n.start()

    pl.semaphore_wait(barrier, n - 1)

    def forward_copy(q):
        return pltpu.make_async_remote_copy(
            src_ref=outgoing.at[q],
            dst_ref=received.at[pl.ds(pl.multiple_of(me * rank, rank), rank)],
            send_sem=send1,
            recv_sem=recv1,
            device_id=(q,),
            device_id_type=MESH,
        )

    def peer(step):
        x, z, y, core = me // 32, me // 8 % 4, me // 2 % 4, me % 2
        dx, dz, dy, dc = step
        return (((x + dx) % (n // 32) * 4 + (z + dz) % 4) * 4 + (y + dy) % 4) * 2 + (core + dc) % 2

    for step in near_first(n):
        q = peer(step)
        outgoing[q] = coef[target(q)]
        forward_copy(q).start()
    received[pl.ds(pl.multiple_of(me * rank, rank), rank), :] = coef[target(me)]

    to_next = pltpu.make_async_remote_copy(
        src_ref=xext.at[pl.ds(leaves, HALO)],
        dst_ref=xext.at[pl.ds(0, HALO)],
        send_sem=hsend.at[0],
        recv_sem=hrecv.at[0],
        device_id=(lax.rem(me + 1, n),),
        device_id_type=MESH,
    )
    to_prior = pltpu.make_async_remote_copy(
        src_ref=xext.at[pl.ds(HALO, HALO)],
        dst_ref=xext.at[pl.ds(HALO + leaves, HALO)],
        send_sem=hsend.at[1],
        recv_sem=hrecv.at[1],
        device_id=(lax.rem(me + n - 1, n),),
        device_id_type=MESH,
    )
    has_next = me < n - 1
    has_prior = me > 0

    @pl.when(has_next)
    def _():
        to_next.start()

    @pl.when(has_prior)
    def _():
        to_prior.start()

    @pl.when(jnp.logical_not(has_prior))
    def _():
        xext[0:HALO] = jnp.zeros((HALO, leaf, rhs), BF16)

    @pl.when(jnp.logical_not(has_next))
    def _():
        xext[HALO + leaves :] = jnp.zeros((HALO, leaf, rhs), BF16)

    for pair in range(leaves // 2):
        rows = []
        for g in (2 * pair, 2 * pair + 1):
            for odd in range(2):
                rows.append(coef_f[g, pl.ds(odd, half, stride=2), :])
        tile = jnp.concatenate(rows, axis=0)
        coef_t[:, pair * 2 * rank : (pair + 1) * 2 * rank] = tile.T.astype(BF16)

    chains(keys, prev_v, last_v, parts, id_parts)
    prev_load = pltpu.make_async_copy(prev_v, prev_s, load_sem.at[4])
    last_load = pltpu.make_async_copy(last_v, last_s, load_sem.at[5])
    prev_load.start()
    last_load.start()
    prev_load.wait()
    last_load.wait()

    load_s.wait()

    chained[cb] = jnp.zeros((half, 2 * rank), F32)
    plain[cb] = jnp.zeros((half, 2 * rank), BF16)
    rolled[cb] = jnp.zeros((half, 2 * rank), BF16)

    def spread(t, carry):
        for j in range(half):
            piece = blocks[pl.ds(pl.multiple_of(t * 16, 16), 16), j * 2 * rank : (j + 1) * 2 * rank]
            raw[pl.ds(j, 16, stride=half), :] = piece.astype(F32)
        for s in range(16):
            k = t * 16 + s
            value = raw[s * half : (s + 1) * half, :] + chained[at(prev_s, k)]
            chained[k] = value
            plain[k] = value.astype(BF16)
            rolled[k] = pltpu.roll(value, rank, 1).astype(BF16)
        return carry

    lax.fori_loop(0, cb // 16, spread, 0, unroll=1)

    groups = n // 4
    my_group = me // 4
    part = min(16, n // 2)

    def back_copy(q):
        return pltpu.make_async_remote_copy(
            src_ref=sums.at[q],
            dst_ref=back.at[me],
            send_sem=send2,
            recv_sem=recv2.at[me // part],
            device_id=(q,),
            device_id_type=MESH,
        )

    def mirror(i, carry):
        g = lax.rem(my_group + i * 13, groups)
        rows = []
        for r in range(leaves):
            upper, lower = [], []
            for pair in range(2):
                k0 = last_s[g // 4, g % 4 * 4 * leaves + 2 * pair * leaves + r]
                k1 = last_s[g // 4, g % 4 * 4 * leaves + (2 * pair + 1) * leaves + r]
                upper.append(jnp.where(low_half, plain[k0], rolled[k1]))
                lower.append(jnp.where(low_half, rolled[k0], plain[k1]))
            rows.append(jnp.concatenate(upper, axis=1))
            rows.append(jnp.concatenate(lower, axis=1))
        tile = jnp.concatenate(rows, axis=0)
        dense[g] = tile
        product = jnp.dot(coef_t[...], tile, preferred_element_type=F32)
        for pair in range(2):
            part = product[:, pair * 2 * rank : (pair + 1) * 2 * rank]
            top, bottom = part[:rank], part[rank:]
            turned = pltpu.roll(jnp.where(low, bottom, top), rank, 1)
            sums[g * 4 + 2 * pair] = jnp.where(low, top, turned).astype(BF16)
            sums[g * 4 + 2 * pair + 1] = jnp.where(low, turned, bottom).astype(BF16)
        for s in range(4):
            q = g * 4 + s

            @pl.when(q != me)
            def _():
                back_copy(q).start()

            @pl.when(q == me)
            def _():
                back[me] = sums[me]

        return carry

    lax.fori_loop(0, groups, mirror, 0, unroll=2)

    for g in range(leaves):
        x_t[g] = xext[HALO + g].astype(F32).T.astype(BF16)
        basis_t[g] = basis[g].astype(F32).T.astype(BF16)

    @pl.when(has_prior)
    def _():
        to_next.wait_recv()

    @pl.when(has_next)
    def _():
        to_prior.wait_recv()

    load_n.wait()
    work[nb] = jnp.zeros((leaf, rhs), F32)

    def near_rows(k, carry):
        y = jnp.dot(near[k], xext[jnp.maximum(at(key_ref, kprev + k) - klast, 0)], preferred_element_type=F32)
        work[k] = y + work[at(prev_s, rprev + k)]
        return carry

    lax.fori_loop(0, nb, near_rows, 0, unroll=8)
    for g in range(leaves):
        near_sum[g] = work[at(last_s, rlast + g)]

    def near_cols(k, carry):
        y = jnp.dot(x_t[jnp.maximum(at(key_ref, rprev + k) - rlast, 0)], near[k], preferred_element_type=F32)
        before = work[at(prev_s, kprev + k)]
        for h in range(2):
            rows = slice(h * rhs, (h + 1) * rhs)
            work[k, rows, :] = y[:, rows] + before[rows]
        return carry

    lax.fori_loop(0, nb, near_cols, 0, unroll=8)

    def spread_of(c):
        return work[at(last_s, klast + c)]

    for h in range(HALO):
        rim_out[0, h] = spread_of(h).astype(BF16)
        rim_out[1, h] = spread_of(HALO + leaves + h).astype(BF16)
    rim_prior = pltpu.make_async_remote_copy(
        src_ref=rim_out.at[0],
        dst_ref=rim_in.at[0],
        send_sem=rsend.at[0],
        recv_sem=rrecv.at[0],
        device_id=(lax.rem(me + n - 1, n),),
        device_id_type=MESH,
    )
    rim_next = pltpu.make_async_remote_copy(
        src_ref=rim_out.at[1],
        dst_ref=rim_in.at[1],
        send_sem=rsend.at[1],
        recv_sem=rrecv.at[1],
        device_id=(lax.rem(me + 1, n),),
        device_id_type=MESH,
    )

    @pl.when(has_prior)
    def _():
        rim_prior.start()

    @pl.when(has_next)
    def _():
        rim_next.start()

    def add_turned(g, y):
        for h in range(2):
            rows = slice(h * rhs, (h + 1) * rhs)
            near_sum[g, rows, :] += y[rows].T

    for g in range(leaves):
        add_turned(g, spread_of(HALO + g))

    others = pl.ds(0, (n - 1) * rank)
    all_forward = pltpu.make_async_remote_copy(
        src_ref=received.at[others],
        dst_ref=received.at[others],
        send_sem=send1,
        recv_sem=recv1,
        device_id=(lax.rem(me + 1, n),),
        device_id_type=MESH,
    )
    all_forward.wait_recv()
    all_forward.wait_send()
    total[...] = jnp.zeros_like(total)
    step = min(4, groups)

    def forward(i, carry):
        acc = total[...]
        for s in range(step):
            g = i * step + s
            c = received[pl.ds(pl.multiple_of(g * 4 * rank, 4 * rank), 4 * rank), :]
            acc = acc + jnp.dot(dense[g], c, preferred_element_type=F32)
        total[...] = acc
        return carry

    lax.fori_loop(0, groups // step, forward, 0)

    @pl.when(has_next)
    def _():
        rim_prior.wait_recv()
        for h in range(HALO):
            add_turned(leaves - HALO + h, rim_in[0, h].astype(F32))

    @pl.when(has_prior)
    def _():
        rim_next.wait_recv()
        for h in range(HALO):
            add_turned(h, rim_in[1, h].astype(F32))

    back_sum[n] = jnp.zeros((rank, rhs), F32)

    def arrived(i, count):
        return pltpu.make_async_remote_copy(
            src_ref=back.at[pl.ds(0, count)],
            dst_ref=back.at[pl.ds(0, count)],
            send_sem=send2,
            recv_sem=recv2.at[i],
            device_id=(lax.rem(me + 1, n),),
            device_id_type=MESH,
        )

    def returned(i, carry):
        @pl.when(me // part == i)
        def _():
            arrived(i, part - 1).wait_recv()

        @pl.when(me // part != i)
        def _():
            arrived(i, part).wait_recv()

        for s in range(part):
            q = i * part + s
            back_sum[q] = back[q].astype(F32) + back_sum[at(prev_s, qprev + q)]
        return carry

    lax.fori_loop(0, n // part, returned, 0)
    arrived(0, n - 1).wait_send()

    def store(g):
        return pltpu.make_async_copy(out.at[g], out_hbm.at[g], load_sem.at[6 + g])

    for g in range(leaves):
        y = back_sum[at(last_s, qlast + g)]
        turned = jnp.concatenate([y, pltpu.roll(y, rank, 1)], axis=0).T
        far_f[g, pl.ds(0, half, stride=2), :] = total[g * rank : g * rank + half, :]
        far_f[g, pl.ds(1, half, stride=2), :] = total[g * rank + half : (g + 1) * rank, :]
        far = (far_f[g] + turned[:rank]).astype(BF16)
        down = jnp.dot(basis_t[g], far, preferred_element_type=F32)
        out[g] = (down + near_sum[g]).astype(BF16)
        store(g).start()

    @pl.when(has_next)
    def _():
        to_next.wait_send()
        rim_next.wait_send()

    @pl.when(has_prior)
    def _():
        to_prior.wait_send()
        rim_prior.wait_send()

    for g in range(leaves):
        store(g).wait()


def per_device(
    features,
    basis_t,
    send_list,
    couple_rows,
    couple_cols,
    couple_blocks,
    near_rows,
    near_cols,
    near_blocks,
):
    n = lax.axis_size("clus")
    leaves, rank, leaf = basis_t.shape
    rhs = features.shape[1]
    cb, nb = couple_blocks.shape[0], near_blocks.shape[0]
    send = send_list.reshape(-1)
    base = -(-n * leaves // 128) * 128
    keys = jnp.concatenate(
        [
            couple_cols * leaves + couple_rows,
            near_rows + base,
            near_cols + (base + leaves),
            send + (base + 2 * leaves + 2 * HALO),
        ]
    )
    keys = jnp.pad(keys, (0, -keys.shape[0] % 128), constant_values=-1).reshape(-1, 128)
    key_rows = keys.shape[0]
    half = rank // 2
    wide = leaves + 2 * HALO
    dma = pltpu.SemaphoreType.DMA
    smem = pl.BlockSpec(memory_space=pltpu.SMEM)
    anywhere = pl.BlockSpec(memory_space=pl.ANY)
    return pl.pallas_call(
        functools.partial(kernel, n, leaves, rank, leaf, rhs, cb, nb),
        out_shape=jax.ShapeDtypeStruct((leaves, leaf, rhs), BF16),
        in_specs=[smem, pl.BlockSpec(memory_space=pltpu.VMEM)] + [anywhere] * 4,
        out_specs=anywhere,
        scratch_shapes=[
            pltpu.VMEM((wide, leaf, rhs), BF16),
            pltpu.VMEM((leaves, rank, leaf), BF16),
            pltpu.VMEM((leaves, leaf, rank), BF16),
            pltpu.VMEM(couple_blocks.shape, BF16),
            pltpu.VMEM(near_blocks.shape, BF16),
            pltpu.VMEM((leaves, rank, rhs), BF16),
            pltpu.VMEM((leaves, rank, rhs), F32),
            pltpu.VMEM((rhs, leaves * rank), BF16),
            pltpu.VMEM((leaves, rhs, leaf), BF16),
            pltpu.VMEM((n, rank, rhs), BF16),
            pltpu.VMEM((n * rank, rhs), BF16),
            pltpu.VMEM((cb + 1, half, 2 * rank), BF16),
            pltpu.VMEM((cb + 1, half, 2 * rank), BF16),
            pltpu.VMEM((n // 4, leaves * rank, 4 * rank), BF16),
            pltpu.VMEM((n, rank, rhs), BF16),
            pltpu.VMEM((n, rank, rhs), BF16),
            pltpu.VMEM((leaves * rank, rhs), F32),
            pltpu.VMEM((16 * half, 2 * rank), F32),
            pltpu.VMEM((cb + 1, half, 2 * rank), F32),
            pltpu.VMEM((nb + 1, leaf, rhs), F32),
            pltpu.VMEM((n + 1, rank, rhs), F32),
            pltpu.VMEM((leaves, leaf, rhs), F32),
            pltpu.VMEM((2, HALO, leaf, rhs), BF16),
            pltpu.VMEM((2, HALO, leaf, rhs), BF16),
            pltpu.VMEM((leaves, leaf, rhs), BF16),
            pltpu.VMEM((leaves, rank, rhs), F32),
            pltpu.VMEM((key_rows, 128), jnp.int32),
            pltpu.VMEM((base // 128 + 1, 128), jnp.int32),
            pltpu.SMEM((key_rows, 128), jnp.int32),
            pltpu.SMEM((base // 128 + 1, 128), jnp.int32),
            dma((6 + leaves,)),
            dma,
            dma,
            dma,
            dma((n // min(16, n // 2),)),
            dma((2,)),
            dma((2,)),
            dma((2,)),
            dma((2,)),
        ],
        compiler_params=pltpu.CompilerParams(
            collective_id=0, has_side_effects=True, vmem_limit_bytes=60 * 1024 * 1024
        ),
    )(
        keys,
        keys,
        features.reshape(leaves, leaf, rhs),
        basis_t,
        couple_blocks,
        near_blocks,
    ).reshape(features.shape)


def solution(mesh):
    placed = (
        P("clus", None),
        P("clus", None, None),
        P("clus", None, None),
        P("clus"),
        P("clus"),
        P("clus", None),
        P("clus"),
        P("clus"),
        P("clus", None, None),
    )
    return jax.shard_map(
        per_device, mesh=mesh, in_specs=placed, out_specs=P("clus", None), check_vma=False
    )
```

```python
import functools
import random

import jax
import jax.numpy as jnp
from jax import lax
from jax.experimental import pallas as pl
from jax.experimental.pallas import tpu as pltpu
from jax.sharding import PartitionSpec as P

HALO = 2
MESH = pl.DeviceIdType.MESH
F32 = jnp.float32
BF16 = jnp.bfloat16


def chains(keys_ref, prev_ref, last_ref, parts, id_parts):
    blocks = keys_ref.shape[0]
    row = lax.broadcasted_iota(jnp.int32, (128, 128), 0)
    col = lax.broadcasted_iota(jnp.int32, (128, 128), 1)
    down = [jnp.broadcast_to(keys_ref[b : b + 1, :], (128, 128)).T for b in range(blocks)]
    lane = lax.broadcasted_iota(jnp.int32, (1, 128), 1)

    def settle(found, place, bounds):
        start, length = jnp.zeros_like(place), jnp.zeros_like(place)
        for first, (at, size) in bounds:
            start = jnp.where(place >= first, at, start)
            length = jnp.where(place >= first, size, length)
        return jnp.where(found < 0, length, jnp.clip(found - start, 0, length))

    for b in range(blocks):
        key = keys_ref[b : b + 1, :]
        best = jnp.full((128, 128), -1, jnp.int32)
        for other in range(b + 1):
            hit = down[other] == key
            if other == b:
                hit = hit & (row < col)
            best = jnp.where(hit, row + other * 128, best)
        found = jnp.max(best, axis=0, keepdims=True)
        prev_ref[b : b + 1, :] = settle(found, lane + b * 128, [(start, (start, size)) for start, size in parts])
    for b in range(last_ref.shape[0]):
        best = jnp.full((128, 128), -1, jnp.int32)
        for other in range(blocks):
            best = jnp.where(down[other] == lane + b * 128, row + other * 128, best)
        found = jnp.max(best, axis=0, keepdims=True)
        last_ref[b : b + 1, :] = settle(found, lane + b * 128, [(first, parts[part]) for first, part in id_parts])


def pass_on(src, dst, sems):
    copies = [pltpu.make_async_copy(src.at[g], dst.at[g], sems.at[g]) for g in range(src.shape[0])]
    for copy in copies:
        copy.start()
    for copy in copies:
        copy.wait()


def near_first(n):
    steps = [(o // 32, o // 8 % 4, o // 2 % 4, o % 2) for o in range(1, n)]
    random.Random(0).shuffle(steps)
    steps.sort(key=lambda o: sum(min(v, 4 - v) for v in o[:3]))
    return steps


def kernel(
    n,
    leaves,
    rank,
    leaf,
    rhs,
    cb,
    nb,
    send_ref,
    nrows_ref,
    ncols_ref,
    rows_v,
    cols_v,
    nrows_v,
    ncols_v,
    send_v,
    x_hbm,
    basis_hbm,
    blocks_hbm,
    near_hbm,
    out_hbm,
    xext,
    basis,
    basis_t,
    blocks,
    near,
    coef,
    coef_f,
    coef_t,
    x_t,
    outgoing,
    received,
    plain,
    rolled,
    dense,
    sums,
    back,
    total,
    raw,
    chained,
    work,
    back_sum,
    near_sum,
    rim_out,
    rim_in,
    out,
    far_f,
    keys,
    prev_v,
    last_v,
    prev_s,
    last_s,
    load_sem,
    send1,
    recv1,
    send2,
    recv2,
    hsend,
    hrecv,
    rsend,
    rrecv,
):
    me = lax.axis_index("clus")
    base = last_v.shape[0] * 128 - 128
    rprev = rows_v.shape[0] * 128
    kprev, qprev = rprev + 128, rprev + 256
    rlast, klast, qlast = base, base + leaves, base + 2 * leaves + 2 * HALO
    parts = [(0, cb), (rprev, nb), (kprev, nb), (qprev, n)]
    id_parts = [(0, 0), (rlast, 1), (klast, 2), (qlast, 3)]

    def at(ref, i):
        return ref[i // 128, i % 128]

    def target(q):
        return send_ref[q]

    half = rank // 2
    lane = lax.broadcasted_iota(jnp.int32, (rank, 2 * rank), 1)
    low = lane < rank
    low_half = lax.broadcasted_iota(jnp.int32, (half, 2 * rank), 1) < rank

    barrier = pltpu.get_barrier_semaphore()

    load_x = pltpu.make_async_copy(x_hbm, xext.at[pl.ds(HALO, leaves)], load_sem.at[0])
    load_b = pltpu.make_async_copy(basis_hbm, basis, load_sem.at[1])
    load_s = pltpu.make_async_copy(blocks_hbm, blocks, load_sem.at[2])
    load_n = pltpu.make_async_copy(near_hbm, near, load_sem.at[3])
    load_x.start()
    load_b.start()

    def greet(i, carry):
        q = lax.rem(me + i, n)
        pl.semaphore_signal(barrier, inc=1, device_id=(q,), device_id_type=MESH)
        return carry

    lax.fori_loop(1, n, greet, 0)

    load_x.wait()
    load_b.wait()
    load_s.start()

    def coefficients(g, carry):
        c = jnp.dot(basis[g], xext[HALO + g], preferred_element_type=F32).astype(BF16)
        coef[g] = c
        coef_f[g] = c.astype(F32)
        return carry

    lax.fori_loop(0, leaves, coefficients, 0, unroll=leaves)
    load_n.start()

    pl.semaphore_wait(barrier, n - 1)

    def forward_copy(q):
        return pltpu.make_async_remote_copy(
            src_ref=outgoing.at[q],
            dst_ref=received.at[pl.ds(pl.multiple_of(me * rank, rank), rank)],
            send_sem=send1,
            recv_sem=recv1,
            device_id=(q,),
            device_id_type=MESH,
        )

    def peer(step):
        x, z, y, core = me // 32, me // 8 % 4, me // 2 % 4, me % 2
        dx, dz, dy, dc = step
        return (((x + dx) % (n // 32) * 4 + (z + dz) % 4) * 4 + (y + dy) % 4) * 2 + (core + dc) % 2

    for step in near_first(n):
        q = peer(step)
        outgoing[q] = coef[target(q)]
        forward_copy(q).start()
    received[pl.ds(pl.multiple_of(me * rank, rank), rank), :] = coef[target(me)]

    to_next = pltpu.make_async_remote_copy(
        src_ref=xext.at[pl.ds(leaves, HALO)],
        dst_ref=xext.at[pl.ds(0, HALO)],
        send_sem=hsend.at[0],
        recv_sem=hrecv.at[0],
        device_id=(lax.rem(me + 1, n),),
        device_id_type=MESH,
    )
    to_prior = pltpu.make_async_remote_copy(
        src_ref=xext.at[pl.ds(HALO, HALO)],
        dst_ref=xext.at[pl.ds(HALO + leaves, HALO)],
        send_sem=hsend.at[1],
        recv_sem=hrecv.at[1],
        device_id=(lax.rem(me + n - 1, n),),
        device_id_type=MESH,
    )
    has_next = me < n - 1
    has_prior = me > 0

    @pl.when(has_next)
    def _():
        to_next.start()

    @pl.when(has_prior)
    def _():
        to_prior.start()

    @pl.when(jnp.logical_not(has_prior))
    def _():
        xext[0:HALO] = jnp.zeros((HALO, leaf, rhs), BF16)

    @pl.when(jnp.logical_not(has_next))
    def _():
        xext[HALO + leaves :] = jnp.zeros((HALO, leaf, rhs), BF16)

    for pair in range(leaves // 2):
        rows = []
        for g in (2 * pair, 2 * pair + 1):
            for odd in range(2):
                rows.append(coef_f[g, pl.ds(odd, half, stride=2), :])
        tile = jnp.concatenate(rows, axis=0)
        coef_t[:, pair * 2 * rank : (pair + 1) * 2 * rank] = tile.T.astype(BF16)

    keys[...] = jnp.full(keys.shape, -1, jnp.int32)
    for b in range(rows_v.shape[0]):
        keys[b : b + 1, :] = cols_v[b : b + 1, :] * leaves + rows_v[b : b + 1, :]
    b = rows_v.shape[0]
    keys[b : b + 1, 0:nb] = nrows_v[...] + rlast
    keys[b + 1 : b + 2, 0:nb] = ncols_v[...] + klast
    keys[b + 2 : b + 3, 0:n] = send_v[...] + qlast
    chains(keys, prev_v, last_v, parts, id_parts)
    prev_load = pltpu.make_async_copy(prev_v, prev_s, load_sem.at[4])
    last_load = pltpu.make_async_copy(last_v, last_s, load_sem.at[5])
    prev_load.start()
    last_load.start()
    prev_load.wait()
    last_load.wait()

    load_s.wait()

    chained[cb] = jnp.zeros((half, 2 * rank), F32)
    plain[cb] = jnp.zeros((half, 2 * rank), BF16)
    rolled[cb] = jnp.zeros((half, 2 * rank), BF16)

    def spread(t, carry):
        for j in range(half):
            piece = blocks[pl.ds(pl.multiple_of(t * 16, 16), 16), j * 2 * rank : (j + 1) * 2 * rank]
            raw[pl.ds(j, 16, stride=half), :] = piece.astype(F32)
        for s in range(16):
            k = t * 16 + s
            value = raw[s * half : (s + 1) * half, :] + chained[at(prev_s, k)]
            chained[k] = value
            plain[k] = value.astype(BF16)
            rolled[k] = pltpu.roll(value, rank, 1).astype(BF16)
        return carry

    lax.fori_loop(0, cb // 16, spread, 0, unroll=1)

    groups = n // 4
    my_group = me // 4
    part = min(16, n // 2)

    def back_copy(q):
        return pltpu.make_async_remote_copy(
            src_ref=sums.at[q],
            dst_ref=back.at[me],
            send_sem=send2,
            recv_sem=recv2.at[me // part],
            device_id=(q,),
            device_id_type=MESH,
        )

    def mirror(i, carry):
        g = lax.rem(my_group + i * 13, groups)
        rows = []
        for r in range(leaves):
            upper, lower = [], []
            for pair in range(2):
                k0 = last_s[g // 4, g % 4 * 4 * leaves + 2 * pair * leaves + r]
                k1 = last_s[g // 4, g % 4 * 4 * leaves + (2 * pair + 1) * leaves + r]
                upper.append(jnp.where(low_half, plain[k0], rolled[k1]))
                lower.append(jnp.where(low_half, rolled[k0], plain[k1]))
            rows.append(jnp.concatenate(upper, axis=1))
            rows.append(jnp.concatenate(lower, axis=1))
        tile = jnp.concatenate(rows, axis=0)
        dense[g] = tile
        product = jnp.dot(coef_t[...], tile, preferred_element_type=F32)
        for pair in range(2):
            part = product[:, pair * 2 * rank : (pair + 1) * 2 * rank]
            top, bottom = part[:rank], part[rank:]
            turned = pltpu.roll(jnp.where(low, bottom, top), rank, 1)
            sums[g * 4 + 2 * pair] = jnp.where(low, top, turned).astype(BF16)
            sums[g * 4 + 2 * pair + 1] = jnp.where(low, turned, bottom).astype(BF16)
        for s in range(4):
            q = g * 4 + s

            @pl.when(q != me)
            def _():
                back_copy(q).start()

            @pl.when(q == me)
            def _():
                back[me] = sums[me]

        return carry

    lax.fori_loop(0, groups, mirror, 0, unroll=2)

    for g in range(leaves):
        x_t[g] = xext[HALO + g].astype(F32).T.astype(BF16)
        basis_t[g] = basis[g].astype(F32).T.astype(BF16)

    @pl.when(has_prior)
    def _():
        to_next.wait_recv()

    @pl.when(has_next)
    def _():
        to_prior.wait_recv()

    load_n.wait()
    work[nb] = jnp.zeros((leaf, rhs), F32)

    def near_rows(k, carry):
        y = jnp.dot(near[k], xext[ncols_ref[k]], preferred_element_type=F32)
        work[k] = y + work[at(prev_s, rprev + k)]
        return carry

    lax.fori_loop(0, nb, near_rows, 0, unroll=8)
    for g in range(leaves):
        near_sum[g] = work[at(last_s, rlast + g)]

    def near_cols(k, carry):
        y = jnp.dot(x_t[nrows_ref[k]], near[k], preferred_element_type=F32)
        before = work[at(prev_s, kprev + k)]
        for h in range(2):
            rows = slice(h * rhs, (h + 1) * rhs)
            work[k, rows, :] = y[:, rows] + before[rows]
        return carry

    lax.fori_loop(0, nb, near_cols, 0, unroll=8)

    def spread_of(c):
        return work[at(last_s, klast + c)]

    for h in range(HALO):
        rim_out[0, h] = spread_of(h).astype(BF16)
        rim_out[1, h] = spread_of(HALO + leaves + h).astype(BF16)
    rim_prior = pltpu.make_async_remote_copy(
        src_ref=rim_out.at[0],
        dst_ref=rim_in.at[0],
        send_sem=rsend.at[0],
        recv_sem=rrecv.at[0],
        device_id=(lax.rem(me + n - 1, n),),
        device_id_type=MESH,
    )
    rim_next = pltpu.make_async_remote_copy(
        src_ref=rim_out.at[1],
        dst_ref=rim_in.at[1],
        send_sem=rsend.at[1],
        recv_sem=rrecv.at[1],
        device_id=(lax.rem(me + 1, n),),
        device_id_type=MESH,
    )

    @pl.when(has_prior)
    def _():
        rim_prior.start()

    @pl.when(has_next)
    def _():
        rim_next.start()

    def add_turned(g, y):
        for h in range(2):
            rows = slice(h * rhs, (h + 1) * rhs)
            near_sum[g, rows, :] += y[rows].T

    for g in range(leaves):
        add_turned(g, spread_of(HALO + g))

    others = pl.ds(0, (n - 1) * rank)
    all_forward = pltpu.make_async_remote_copy(
        src_ref=received.at[others],
        dst_ref=received.at[others],
        send_sem=send1,
        recv_sem=recv1,
        device_id=(lax.rem(me + 1, n),),
        device_id_type=MESH,
    )
    all_forward.wait_recv()
    all_forward.wait_send()
    total[...] = jnp.zeros_like(total)
    step = min(4, groups)

    def forward(i, carry):
        acc = total[...]
        for s in range(step):
            g = i * step + s
            c = received[pl.ds(pl.multiple_of(g * 4 * rank, 4 * rank), 4 * rank), :]
            acc = acc + jnp.dot(dense[g], c, preferred_element_type=F32)
        total[...] = acc
        return carry

    lax.fori_loop(0, groups // step, forward, 0)

    @pl.when(has_next)
    def _():
        rim_prior.wait_recv()
        for h in range(HALO):
            add_turned(leaves - HALO + h, rim_in[0, h].astype(F32))

    @pl.when(has_prior)
    def _():
        rim_next.wait_recv()
        for h in range(HALO):
            add_turned(h, rim_in[1, h].astype(F32))

    back_sum[n] = jnp.zeros((rank, rhs), F32)

    def arrived(i, count):
        return pltpu.make_async_remote_copy(
            src_ref=back.at[pl.ds(0, count)],
            dst_ref=back.at[pl.ds(0, count)],
            send_sem=send2,
            recv_sem=recv2.at[i],
            device_id=(lax.rem(me + 1, n),),
            device_id_type=MESH,
        )

    def returned(i, carry):
        @pl.when(me // part == i)
        def _():
            arrived(i, part - 1).wait_recv()

        @pl.when(me // part != i)
        def _():
            arrived(i, part).wait_recv()

        for s in range(part):
            q = i * part + s
            back_sum[q] = back[q].astype(F32) + back_sum[at(prev_s, qprev + q)]
        return carry

    lax.fori_loop(0, n // part, returned, 0)
    arrived(0, n - 1).wait_send()

    def store(g):
        return pltpu.make_async_copy(out.at[g], out_hbm.at[g], load_sem.at[6 + g])

    for g in range(leaves):
        y = back_sum[at(last_s, qlast + g)]
        turned = jnp.concatenate([y, pltpu.roll(y, rank, 1)], axis=0).T
        far_f[g, pl.ds(0, half, stride=2), :] = total[g * rank : g * rank + half, :]
        far_f[g, pl.ds(1, half, stride=2), :] = total[g * rank + half : (g + 1) * rank, :]
        far = (far_f[g] + turned[:rank]).astype(BF16)
        down = jnp.dot(basis_t[g], far, preferred_element_type=F32)
        out[g] = (down + near_sum[g]).astype(BF16)
        store(g).start()

    @pl.when(has_next)
    def _():
        to_next.wait_send()
        rim_next.wait_send()

    @pl.when(has_prior)
    def _():
        to_prior.wait_send()
        rim_prior.wait_send()

    for g in range(leaves):
        store(g).wait()


def per_device(
    features,
    basis_t,
    send_list,
    couple_rows,
    couple_cols,
    couple_blocks,
    near_rows,
    near_cols,
    near_blocks,
):
    n = lax.axis_size("clus")
    leaves, rank, leaf = basis_t.shape
    rhs = features.shape[1]
    cb, nb = couple_blocks.shape[0], near_blocks.shape[0]
    send = send_list.reshape(-1)
    base = -(-n * leaves // 128) * 128
    key_rows = cb // 128 + 3
    half = rank // 2
    wide = leaves + 2 * HALO
    dma = pltpu.SemaphoreType.DMA
    smem = pl.BlockSpec(memory_space=pltpu.SMEM)
    anywhere = pl.BlockSpec(memory_space=pl.ANY)
    result = pl.pallas_call(
        functools.partial(kernel, n, leaves, rank, leaf, rhs, cb, nb),
        out_shape=jax.ShapeDtypeStruct((leaves, leaf, rhs), BF16),
        in_specs=[smem] * 3 + [pl.BlockSpec(memory_space=pltpu.VMEM)] * 5 + [anywhere] * 4,
        out_specs=anywhere,
        scratch_shapes=[
            pltpu.VMEM((wide, leaf, rhs), BF16),
            pltpu.VMEM((leaves, rank, leaf), BF16),
            pltpu.VMEM((leaves, leaf, rank), BF16),
            pltpu.VMEM(couple_blocks.shape, BF16),
            pltpu.VMEM(near_blocks.shape, BF16),
            pltpu.VMEM((leaves, rank, rhs), BF16),
            pltpu.VMEM((leaves, rank, rhs), F32),
            pltpu.VMEM((rhs, leaves * rank), BF16),
            pltpu.VMEM((leaves, rhs, leaf), BF16),
            pltpu.VMEM((n, rank, rhs), BF16),
            pltpu.VMEM((n * rank, rhs), BF16),
            pltpu.VMEM((cb + 1, half, 2 * rank), BF16),
            pltpu.VMEM((cb + 1, half, 2 * rank), BF16),
            pltpu.VMEM((n // 4, leaves * rank, 4 * rank), BF16),
            pltpu.VMEM((n, rank, rhs), BF16),
            pltpu.VMEM((n, rank, rhs), BF16),
            pltpu.VMEM((leaves * rank, rhs), F32),
            pltpu.VMEM((16 * half, 2 * rank), F32),
            pltpu.VMEM((cb + 1, half, 2 * rank), F32),
            pltpu.VMEM((nb + 1, leaf, rhs), F32),
            pltpu.VMEM((n + 1, rank, rhs), F32),
            pltpu.VMEM((leaves, leaf, rhs), F32),
            pltpu.VMEM((2, HALO, leaf, rhs), BF16),
            pltpu.VMEM((2, HALO, leaf, rhs), BF16),
            pltpu.VMEM((leaves, leaf, rhs), BF16),
            pltpu.VMEM((leaves, rank, rhs), F32),
            pltpu.VMEM((key_rows, 128), jnp.int32),
            pltpu.VMEM((key_rows, 128), jnp.int32),
            pltpu.VMEM((base // 128 + 1, 128), jnp.int32),
            pltpu.SMEM((key_rows, 128), jnp.int32),
            pltpu.SMEM((base // 128 + 1, 128), jnp.int32),
            dma((6 + leaves,)),
            dma,
            dma,
            dma,
            dma((n // min(16, n // 2),)),
            dma((2,)),
            dma((2,)),
            dma((2,)),
            dma((2,)),
        ],
        compiler_params=pltpu.CompilerParams(
            collective_id=0, has_side_effects=True, vmem_limit_bytes=60 * 1024 * 1024
        ),
    )(
        send,
        near_rows,
        near_cols,
        couple_rows.reshape(-1, 128),
        couple_cols.reshape(-1, 128),
        near_rows.reshape(1, nb),
        near_cols.reshape(1, nb),
        send.reshape(1, n),
        features.reshape(leaves, leaf, rhs),
        basis_t,
        couple_blocks,
        near_blocks,
    )
    return pl.pallas_call(
        pass_on,
        out_shape=jax.ShapeDtypeStruct(result.shape, BF16),
        in_specs=[anywhere],
        out_specs=anywhere,
        scratch_shapes=[dma((leaves,))],
    )(result).reshape(features.shape)


def solution(mesh):
    placed = (
        P("clus", None),
        P("clus", None, None),
        P("clus", None, None),
        P("clus"),
        P("clus"),
        P("clus", None),
        P("clus"),
        P("clus"),
        P("clus", None, None),
    )
    return jax.shard_map(
        per_device, mesh=mesh, in_specs=placed, out_specs=P("clus", None), check_vma=False
    )
```

```python
import functools
import random

import jax
import jax.numpy as jnp
from jax import lax
from jax.experimental import pallas as pl
from jax.experimental.pallas import tpu as pltpu
from jax.sharding import PartitionSpec as P

HALO = 2
MESH = pl.DeviceIdType.MESH
F32 = jnp.float32
BF16 = jnp.bfloat16


def chains(keys_ref, prev_ref, last_ref, parts, id_parts):
    blocks = keys_ref.shape[0]
    row = lax.broadcasted_iota(jnp.int32, (128, 128), 0)
    col = lax.broadcasted_iota(jnp.int32, (128, 128), 1)
    down = [jnp.broadcast_to(keys_ref[b : b + 1, :], (128, 128)).T for b in range(blocks)]
    lane = lax.broadcasted_iota(jnp.int32, (1, 128), 1)

    def settle(found, place, bounds):
        start, length = jnp.zeros_like(place), jnp.zeros_like(place)
        for first, (at, size) in bounds:
            start = jnp.where(place >= first, at, start)
            length = jnp.where(place >= first, size, length)
        return jnp.where(found < 0, length, jnp.clip(found - start, 0, length))

    for b in range(blocks):
        key = keys_ref[b : b + 1, :]
        best = jnp.full((128, 128), -1, jnp.int32)
        for other in range(b + 1):
            hit = down[other] == key
            if other == b:
                hit = hit & (row < col)
            best = jnp.where(hit, row + other * 128, best)
        found = jnp.max(best, axis=0, keepdims=True)
        prev_ref[b : b + 1, :] = settle(found, lane + b * 128, [(start, (start, size)) for start, size in parts])
    for b in range(last_ref.shape[0]):
        best = jnp.full((128, 128), -1, jnp.int32)
        for other in range(blocks):
            best = jnp.where(down[other] == lane + b * 128, row + other * 128, best)
        found = jnp.max(best, axis=0, keepdims=True)
        last_ref[b : b + 1, :] = settle(found, lane + b * 128, [(first, parts[part]) for first, part in id_parts])


def near_first(n):
    steps = [(o // 32, o // 8 % 4, o // 2 % 4, o % 2) for o in range(1, n)]
    random.Random(0).shuffle(steps)
    steps.sort(key=lambda o: sum(min(v, 4 - v) for v in o[:3]))
    return steps


def kernel(
    n,
    leaves,
    rank,
    leaf,
    rhs,
    cb,
    nb,
    send_ref,
    nrows_ref,
    ncols_ref,
    rows_v,
    cols_v,
    nrows_v,
    ncols_v,
    send_v,
    x_hbm,
    basis_hbm,
    blocks_hbm,
    near_hbm,
    out_hbm,
    xext,
    basis,
    basis_t,
    blocks,
    near,
    coef,
    coef_f,
    coef_t,
    x_t,
    outgoing,
    received,
    plain,
    rolled,
    dense,
    sums,
    back,
    total,
    raw,
    chained,
    work,
    back_sum,
    near_sum,
    rim_out,
    rim_in,
    out,
    far_f,
    keys,
    prev_v,
    last_v,
    prev_s,
    last_s,
    load_sem,
    send1,
    recv1,
    send2,
    recv2,
    hsend,
    hrecv,
    rsend,
    rrecv,
):
    me = lax.axis_index("clus")
    base = last_v.shape[0] * 128 - 128
    rprev = rows_v.shape[0] * 128
    kprev, qprev = rprev + 128, rprev + 256
    rlast, klast, qlast = base, base + leaves, base + 2 * leaves + 2 * HALO
    parts = [(0, cb), (rprev, nb), (kprev, nb), (qprev, n)]
    id_parts = [(0, 0), (rlast, 1), (klast, 2), (qlast, 3)]

    def at(ref, i):
        return ref[i // 128, i % 128]

    def target(q):
        return send_ref[q]

    half = rank // 2
    lane = lax.broadcasted_iota(jnp.int32, (rank, 2 * rank), 1)
    low = lane < rank
    low_half = lax.broadcasted_iota(jnp.int32, (half, 2 * rank), 1) < rank

    barrier = pltpu.get_barrier_semaphore()

    load_x = pltpu.make_async_copy(x_hbm, xext.at[pl.ds(HALO, leaves)], load_sem.at[0])
    load_b = pltpu.make_async_copy(basis_hbm, basis, load_sem.at[1])
    load_s = pltpu.make_async_copy(blocks_hbm, blocks, load_sem.at[2])
    load_n = pltpu.make_async_copy(near_hbm, near, load_sem.at[3])
    load_x.start()
    load_b.start()

    def greet(i, carry):
        q = lax.rem(me + i, n)
        pl.semaphore_signal(barrier, inc=1, device_id=(q,), device_id_type=MESH)
        return carry

    lax.fori_loop(1, n, greet, 0)

    load_x.wait()
    load_b.wait()
    load_s.start()

    def coefficients(g, carry):
        c = jnp.dot(basis[g], xext[HALO + g], preferred_element_type=F32).astype(BF16)
        coef[g] = c
        coef_f[g] = c.astype(F32)
        return carry

    lax.fori_loop(0, leaves, coefficients, 0, unroll=leaves)
    load_n.start()

    pl.semaphore_wait(barrier, n - 1)

    def forward_copy(q):
        return pltpu.make_async_remote_copy(
            src_ref=outgoing.at[q],
            dst_ref=received.at[pl.ds(pl.multiple_of(me * rank, rank), rank)],
            send_sem=send1,
            recv_sem=recv1,
            device_id=(q,),
            device_id_type=MESH,
        )

    def peer(step):
        x, z, y, core = me // 32, me // 8 % 4, me // 2 % 4, me % 2
        dx, dz, dy, dc = step
        return (((x + dx) % (n // 32) * 4 + (z + dz) % 4) * 4 + (y + dy) % 4) * 2 + (core + dc) % 2

    for step in near_first(n):
        q = peer(step)
        outgoing[q] = coef[target(q)]
        forward_copy(q).start()
    received[pl.ds(pl.multiple_of(me * rank, rank), rank), :] = coef[target(me)]

    to_next = pltpu.make_async_remote_copy(
        src_ref=xext.at[pl.ds(leaves, HALO)],
        dst_ref=xext.at[pl.ds(0, HALO)],
        send_sem=hsend.at[0],
        recv_sem=hrecv.at[0],
        device_id=(lax.rem(me + 1, n),),
        device_id_type=MESH,
    )
    to_prior = pltpu.make_async_remote_copy(
        src_ref=xext.at[pl.ds(HALO, HALO)],
        dst_ref=xext.at[pl.ds(HALO + leaves, HALO)],
        send_sem=hsend.at[1],
        recv_sem=hrecv.at[1],
        device_id=(lax.rem(me + n - 1, n),),
        device_id_type=MESH,
    )
    has_next = me < n - 1
    has_prior = me > 0

    @pl.when(has_next)
    def _():
        to_next.start()

    @pl.when(has_prior)
    def _():
        to_prior.start()

    @pl.when(jnp.logical_not(has_prior))
    def _():
        xext[0:HALO] = jnp.zeros((HALO, leaf, rhs), BF16)

    @pl.when(jnp.logical_not(has_next))
    def _():
        xext[HALO + leaves :] = jnp.zeros((HALO, leaf, rhs), BF16)

    for pair in range(leaves // 2):
        rows = []
        for g in (2 * pair, 2 * pair + 1):
            for odd in range(2):
                rows.append(coef_f[g, pl.ds(odd, half, stride=2), :])
        tile = jnp.concatenate(rows, axis=0)
        coef_t[:, pair * 2 * rank : (pair + 1) * 2 * rank] = tile.T.astype(BF16)

    keys[...] = jnp.full(keys.shape, -1, jnp.int32)
    for b in range(rows_v.shape[0]):
        keys[b : b + 1, :] = cols_v[b : b + 1, :] * leaves + rows_v[b : b + 1, :]
    b = rows_v.shape[0]
    keys[b : b + 1, 0:nb] = nrows_v[...] + rlast
    keys[b + 1 : b + 2, 0:nb] = ncols_v[...] + klast
    keys[b + 2 : b + 3, 0:n] = send_v[...] + qlast
    chains(keys, prev_v, last_v, parts, id_parts)
    prev_load = pltpu.make_async_copy(prev_v, prev_s, load_sem.at[4])
    last_load = pltpu.make_async_copy(last_v, last_s, load_sem.at[5])
    prev_load.start()
    last_load.start()
    prev_load.wait()
    last_load.wait()

    load_s.wait()

    chained[cb] = jnp.zeros((half, 2 * rank), F32)
    plain[cb] = jnp.zeros((half, 2 * rank), BF16)
    rolled[cb] = jnp.zeros((half, 2 * rank), BF16)

    def spread(t, carry):
        for j in range(half):
            piece = blocks[pl.ds(pl.multiple_of(t * 16, 16), 16), j * 2 * rank : (j + 1) * 2 * rank]
            raw[pl.ds(j, 16, stride=half), :] = piece.astype(F32)
        for s in range(16):
            k = t * 16 + s
            value = raw[s * half : (s + 1) * half, :] + chained[at(prev_s, k)]
            chained[k] = value
            plain[k] = value.astype(BF16)
            rolled[k] = pltpu.roll(value, rank, 1).astype(BF16)
        return carry

    lax.fori_loop(0, cb // 16, spread, 0, unroll=1)

    groups = n // 4
    my_group = me // 4
    part = min(16, n // 2)

    def back_copy(q):
        return pltpu.make_async_remote_copy(
            src_ref=sums.at[q],
            dst_ref=back.at[me],
            send_sem=send2,
            recv_sem=recv2.at[me // part],
            device_id=(q,),
            device_id_type=MESH,
        )

    def mirror(i, carry):
        g = lax.rem(my_group + i * 13, groups)
        rows = []
        for r in range(leaves):
            upper, lower = [], []
            for pair in range(2):
                k0 = last_s[g // 4, g % 4 * 4 * leaves + 2 * pair * leaves + r]
                k1 = last_s[g // 4, g % 4 * 4 * leaves + (2 * pair + 1) * leaves + r]
                upper.append(jnp.where(low_half, plain[k0], rolled[k1]))
                lower.append(jnp.where(low_half, rolled[k0], plain[k1]))
            rows.append(jnp.concatenate(upper, axis=1))
            rows.append(jnp.concatenate(lower, axis=1))
        tile = jnp.concatenate(rows, axis=0)
        dense[g] = tile
        product = jnp.dot(coef_t[...], tile, preferred_element_type=F32)
        for pair in range(2):
            part = product[:, pair * 2 * rank : (pair + 1) * 2 * rank]
            top, bottom = part[:rank], part[rank:]
            turned = pltpu.roll(jnp.where(low, bottom, top), rank, 1)
            sums[g * 4 + 2 * pair] = jnp.where(low, top, turned).astype(BF16)
            sums[g * 4 + 2 * pair + 1] = jnp.where(low, turned, bottom).astype(BF16)
        for s in range(4):
            q = g * 4 + s

            @pl.when(q != me)
            def _():
                back_copy(q).start()

            @pl.when(q == me)
            def _():
                back[me] = sums[me]

        return carry

    lax.fori_loop(0, groups, mirror, 0, unroll=2)

    for g in range(leaves):
        x_t[g] = xext[HALO + g].astype(F32).T.astype(BF16)
        basis_t[g] = basis[g].astype(F32).T.astype(BF16)

    @pl.when(has_prior)
    def _():
        to_next.wait_recv()

    @pl.when(has_next)
    def _():
        to_prior.wait_recv()

    load_n.wait()
    work[nb] = jnp.zeros((leaf, rhs), F32)

    def near_rows(k, carry):
        y = jnp.dot(near[k], xext[ncols_ref[k]], preferred_element_type=F32)
        work[k] = y + work[at(prev_s, rprev + k)]
        return carry

    lax.fori_loop(0, nb, near_rows, 0, unroll=8)
    for g in range(leaves):
        near_sum[g] = work[at(last_s, rlast + g)]

    def near_cols(k, carry):
        y = jnp.dot(x_t[nrows_ref[k]], near[k], preferred_element_type=F32)
        before = work[at(prev_s, kprev + k)]
        for h in range(2):
            rows = slice(h * rhs, (h + 1) * rhs)
            work[k, rows, :] = y[:, rows] + before[rows]
        return carry

    lax.fori_loop(0, nb, near_cols, 0, unroll=8)

    def spread_of(c):
        return work[at(last_s, klast + c)]

    for h in range(HALO):
        rim_out[0, h] = spread_of(h).astype(BF16)
        rim_out[1, h] = spread_of(HALO + leaves + h).astype(BF16)
    rim_prior = pltpu.make_async_remote_copy(
        src_ref=rim_out.at[0],
        dst_ref=rim_in.at[0],
        send_sem=rsend.at[0],
        recv_sem=rrecv.at[0],
        device_id=(lax.rem(me + n - 1, n),),
        device_id_type=MESH,
    )
    rim_next = pltpu.make_async_remote_copy(
        src_ref=rim_out.at[1],
        dst_ref=rim_in.at[1],
        send_sem=rsend.at[1],
        recv_sem=rrecv.at[1],
        device_id=(lax.rem(me + 1, n),),
        device_id_type=MESH,
    )

    @pl.when(has_prior)
    def _():
        rim_prior.start()

    @pl.when(has_next)
    def _():
        rim_next.start()

    def add_turned(g, y):
        for h in range(2):
            rows = slice(h * rhs, (h + 1) * rhs)
            near_sum[g, rows, :] += y[rows].T

    for g in range(leaves):
        add_turned(g, spread_of(HALO + g))

    others = pl.ds(0, (n - 1) * rank)
    all_forward = pltpu.make_async_remote_copy(
        src_ref=received.at[others],
        dst_ref=received.at[others],
        send_sem=send1,
        recv_sem=recv1,
        device_id=(lax.rem(me + 1, n),),
        device_id_type=MESH,
    )
    all_forward.wait_recv()
    all_forward.wait_send()
    total[...] = jnp.zeros_like(total)
    step = min(4, groups)

    def forward(i, carry):
        acc = total[...]
        for s in range(step):
            g = i * step + s
            c = received[pl.ds(pl.multiple_of(g * 4 * rank, 4 * rank), 4 * rank), :]
            acc = acc + jnp.dot(dense[g], c, preferred_element_type=F32)
        total[...] = acc
        return carry

    lax.fori_loop(0, groups // step, forward, 0)

    @pl.when(has_next)
    def _():
        rim_prior.wait_recv()
        for h in range(HALO):
            add_turned(leaves - HALO + h, rim_in[0, h].astype(F32))

    @pl.when(has_prior)
    def _():
        rim_next.wait_recv()
        for h in range(HALO):
            add_turned(h, rim_in[1, h].astype(F32))

    back_sum[n] = jnp.zeros((rank, rhs), F32)

    def arrived(i, count):
        return pltpu.make_async_remote_copy(
            src_ref=back.at[pl.ds(0, count)],
            dst_ref=back.at[pl.ds(0, count)],
            send_sem=send2,
            recv_sem=recv2.at[i],
            device_id=(lax.rem(me + 1, n),),
            device_id_type=MESH,
        )

    def returned(i, carry):
        @pl.when(me // part == i)
        def _():
            arrived(i, part - 1).wait_recv()

        @pl.when(me // part != i)
        def _():
            arrived(i, part).wait_recv()

        for s in range(part):
            q = i * part + s
            back_sum[q] = back[q].astype(F32) + back_sum[at(prev_s, qprev + q)]
        return carry

    lax.fori_loop(0, n // part, returned, 0)
    arrived(0, n - 1).wait_send()

    def store(g):
        return pltpu.make_async_copy(out.at[g], out_hbm.at[g], load_sem.at[6 + g])

    for g in range(leaves):
        y = back_sum[at(last_s, qlast + g)]
        turned = jnp.concatenate([y, pltpu.roll(y, rank, 1)], axis=0).T
        far_f[g, pl.ds(0, half, stride=2), :] = total[g * rank : g * rank + half, :]
        far_f[g, pl.ds(1, half, stride=2), :] = total[g * rank + half : (g + 1) * rank, :]
        far = (far_f[g] + turned[:rank]).astype(BF16)
        down = jnp.dot(basis_t[g], far, preferred_element_type=F32)
        out[g] = (down + near_sum[g]).astype(BF16)
        store(g).start()

    @pl.when(has_next)
    def _():
        to_next.wait_send()
        rim_next.wait_send()

    @pl.when(has_prior)
    def _():
        to_prior.wait_send()
        rim_prior.wait_send()

    for g in range(leaves):
        store(g).wait()


def per_device(
    features,
    basis_t,
    send_list,
    couple_rows,
    couple_cols,
    couple_blocks,
    near_rows,
    near_cols,
    near_blocks,
):
    n = lax.axis_size("clus")
    leaves, rank, leaf = basis_t.shape
    rhs = features.shape[1]
    cb, nb = couple_blocks.shape[0], near_blocks.shape[0]
    send = send_list.reshape(-1)
    base = -(-n * leaves // 128) * 128
    key_rows = cb // 128 + 3
    half = rank // 2
    wide = leaves + 2 * HALO
    dma = pltpu.SemaphoreType.DMA
    smem = pl.BlockSpec(memory_space=pltpu.SMEM)
    anywhere = pl.BlockSpec(memory_space=pl.ANY)
    return pl.pallas_call(
        functools.partial(kernel, n, leaves, rank, leaf, rhs, cb, nb),
        out_shape=jax.ShapeDtypeStruct((leaves, leaf, rhs), BF16),
        in_specs=[smem] * 3 + [pl.BlockSpec(memory_space=pltpu.VMEM)] * 5 + [anywhere] * 4,
        out_specs=anywhere,
        scratch_shapes=[
            pltpu.VMEM((wide, leaf, rhs), BF16),
            pltpu.VMEM((leaves, rank, leaf), BF16),
            pltpu.VMEM((leaves, leaf, rank), BF16),
            pltpu.VMEM(couple_blocks.shape, BF16),
            pltpu.VMEM(near_blocks.shape, BF16),
            pltpu.VMEM((leaves, rank, rhs), BF16),
            pltpu.VMEM((leaves, rank, rhs), F32),
            pltpu.VMEM((rhs, leaves * rank), BF16),
            pltpu.VMEM((leaves, rhs, leaf), BF16),
            pltpu.VMEM((n, rank, rhs), BF16),
            pltpu.VMEM((n * rank, rhs), BF16),
            pltpu.VMEM((cb + 1, half, 2 * rank), BF16),
            pltpu.VMEM((cb + 1, half, 2 * rank), BF16),
            pltpu.VMEM((n // 4, leaves * rank, 4 * rank), BF16),
            pltpu.VMEM((n, rank, rhs), BF16),
            pltpu.VMEM((n, rank, rhs), BF16),
            pltpu.VMEM((leaves * rank, rhs), F32),
            pltpu.VMEM((16 * half, 2 * rank), F32),
            pltpu.VMEM((cb + 1, half, 2 * rank), F32),
            pltpu.VMEM((nb + 1, leaf, rhs), F32),
            pltpu.VMEM((n + 1, rank, rhs), F32),
            pltpu.VMEM((leaves, leaf, rhs), F32),
            pltpu.VMEM((2, HALO, leaf, rhs), BF16),
            pltpu.VMEM((2, HALO, leaf, rhs), BF16),
            pltpu.VMEM((leaves, leaf, rhs), BF16),
            pltpu.VMEM((leaves, rank, rhs), F32),
            pltpu.VMEM((key_rows, 128), jnp.int32),
            pltpu.VMEM((key_rows, 128), jnp.int32),
            pltpu.VMEM((base // 128 + 1, 128), jnp.int32),
            pltpu.SMEM((key_rows, 128), jnp.int32),
            pltpu.SMEM((base // 128 + 1, 128), jnp.int32),
            dma((6 + leaves,)),
            dma,
            dma,
            dma,
            dma((n // min(16, n // 2),)),
            dma((2,)),
            dma((2,)),
            dma((2,)),
            dma((2,)),
        ],
        compiler_params=pltpu.CompilerParams(
            collective_id=0, has_side_effects=True, vmem_limit_bytes=60 * 1024 * 1024
        ),
    )(
        send,
        near_rows,
        near_cols,
        couple_rows.reshape(-1, 128),
        couple_cols.reshape(-1, 128),
        near_rows.reshape(1, nb),
        near_cols.reshape(1, nb),
        send.reshape(1, n),
        features.reshape(leaves, leaf, rhs),
        basis_t,
        couple_blocks,
        near_blocks,
    ).reshape(features.shape)


def solution(mesh):
    placed = (
        P("clus", None),
        P("clus", None, None),
        P("clus", None, None),
        P("clus"),
        P("clus"),
        P("clus", None),
        P("clus"),
        P("clus"),
        P("clus", None, None),
    )
    return jax.shard_map(
        per_device, mesh=mesh, in_specs=placed, out_specs=P("clus", None), check_vma=False
    )
```

```python
import functools
import random

import jax
import jax.numpy as jnp
from jax import lax
from jax.experimental import pallas as pl
from jax.experimental.pallas import tpu as pltpu
from jax.sharding import PartitionSpec as P

HALO = 2
MESH = pl.DeviceIdType.MESH
F32 = jnp.float32
BF16 = jnp.bfloat16


def chains(keys_ref, prev_ref, last_ref, parts, id_parts):
    blocks = keys_ref.shape[0]
    row = lax.broadcasted_iota(jnp.int32, (128, 128), 0)
    col = lax.broadcasted_iota(jnp.int32, (128, 128), 1)
    down = [jnp.broadcast_to(keys_ref[b : b + 1, :], (128, 128)).T for b in range(blocks)]
    lane = lax.broadcasted_iota(jnp.int32, (1, 128), 1)

    def settle(found, place, bounds):
        start, length = jnp.zeros_like(place), jnp.zeros_like(place)
        for first, (at, size) in bounds:
            start = jnp.where(place >= first, at, start)
            length = jnp.where(place >= first, size, length)
        return jnp.where(found < 0, length, jnp.clip(found - start, 0, length))

    for b in range(blocks):
        key = keys_ref[b : b + 1, :]
        best = jnp.full((128, 128), -1, jnp.int32)
        for other in range(b + 1):
            hit = down[other] == key
            if other == b:
                hit = hit & (row < col)
            best = jnp.where(hit, row + other * 128, best)
        found = jnp.max(best, axis=0, keepdims=True)
        prev_ref[b : b + 1, :] = settle(found, lane + b * 128, [(start, (start, size)) for start, size in parts])
    for b in range(last_ref.shape[0]):
        best = jnp.full((128, 128), -1, jnp.int32)
        for other in range(blocks):
            best = jnp.where(down[other] == lane + b * 128, row + other * 128, best)
        found = jnp.max(best, axis=0, keepdims=True)
        last_ref[b : b + 1, :] = settle(found, lane + b * 128, [(first, parts[part]) for first, part in id_parts])


def near_first(n):
    steps = [(o // 32, o // 8 % 4, o // 2 % 4, o % 2) for o in range(1, n)]
    random.Random(0).shuffle(steps)
    steps.sort(key=lambda o: sum(min(v, 4 - v) for v in o[:3]))
    return steps


def kernel(
    n,
    leaves,
    rank,
    leaf,
    rhs,
    cb,
    nb,
    send_ref,
    nrows_ref,
    ncols_ref,
    rows_v,
    cols_v,
    nrows_v,
    ncols_v,
    send_v,
    x_hbm,
    basis_hbm,
    blocks_hbm,
    near_hbm,
    out_hbm,
    xext,
    basis,
    basis_t,
    blocks,
    near,
    coef,
    coef_f,
    coef_t,
    x_t,
    outgoing,
    received,
    plain,
    rolled,
    dense,
    sums,
    back,
    total,
    raw,
    chained,
    work,
    back_sum,
    near_sum,
    rim_out,
    rim_in,
    out,
    far_f,
    keys,
    prev_v,
    last_v,
    prev_s,
    last_s,
    load_sem,
    send1,
    recv1,
    send2,
    recv2,
    hsend,
    hrecv,
    rsend,
    rrecv,
):
    me = lax.axis_index("clus")
    base = last_v.shape[0] * 128 - 128
    rprev = rows_v.shape[0] * 128
    kprev, qprev = rprev + 128, rprev + 256
    rlast, klast, qlast = base, base + leaves, base + 2 * leaves + 2 * HALO
    parts = [(0, cb), (rprev, nb), (kprev, nb), (qprev, n)]
    id_parts = [(0, 0), (rlast, 1), (klast, 2), (qlast, 3)]

    def at(ref, i):
        return ref[i // 128, i % 128]

    def target(q):
        return send_ref[q]

    half = rank // 2
    lane = lax.broadcasted_iota(jnp.int32, (rank, 2 * rank), 1)
    low = lane < rank
    low_half = lax.broadcasted_iota(jnp.int32, (half, 2 * rank), 1) < rank

    barrier = pltpu.get_barrier_semaphore()

    load_x = pltpu.make_async_copy(x_hbm, xext.at[pl.ds(HALO, leaves)], load_sem.at[0])
    load_b = pltpu.make_async_copy(basis_hbm, basis, load_sem.at[1])
    load_s = pltpu.make_async_copy(blocks_hbm, blocks, load_sem.at[2])
    load_n = pltpu.make_async_copy(near_hbm, near, load_sem.at[3])
    load_x.start()
    load_b.start()

    def greet(i, carry):
        q = lax.rem(me + i, n)
        pl.semaphore_signal(barrier, inc=1, device_id=(q,), device_id_type=MESH)
        return carry

    lax.fori_loop(1, n, greet, 0)

    load_x.wait()
    load_b.wait()
    load_s.start()

    def coefficients(g, carry):
        c = jnp.dot(basis[g], xext[HALO + g], preferred_element_type=F32).astype(BF16)
        coef[g] = c
        coef_f[g] = c.astype(F32)
        return carry

    lax.fori_loop(0, leaves, coefficients, 0, unroll=leaves)
    load_n.start()

    pl.semaphore_wait(barrier, n - 1)

    def forward_copy(q):
        return pltpu.make_async_remote_copy(
            src_ref=outgoing.at[q],
            dst_ref=received.at[pl.ds(pl.multiple_of(me * rank, rank), rank)],
            send_sem=send1,
            recv_sem=recv1,
            device_id=(q,),
            device_id_type=MESH,
        )

    def peer(step):
        x, z, y, core = me // 32, me // 8 % 4, me // 2 % 4, me % 2
        dx, dz, dy, dc = step
        return (((x + dx) % (n // 32) * 4 + (z + dz) % 4) * 4 + (y + dy) % 4) * 2 + (core + dc) % 2

    for step in near_first(n):
        q = peer(step)
        outgoing[q] = coef[target(q)]
        forward_copy(q).start()
    received[pl.ds(pl.multiple_of(me * rank, rank), rank), :] = coef[target(me)]

    to_next = pltpu.make_async_remote_copy(
        src_ref=xext.at[pl.ds(leaves, HALO)],
        dst_ref=xext.at[pl.ds(0, HALO)],
        send_sem=hsend.at[0],
        recv_sem=hrecv.at[0],
        device_id=(lax.rem(me + 1, n),),
        device_id_type=MESH,
    )
    to_prior = pltpu.make_async_remote_copy(
        src_ref=xext.at[pl.ds(HALO, HALO)],
        dst_ref=xext.at[pl.ds(HALO + leaves, HALO)],
        send_sem=hsend.at[1],
        recv_sem=hrecv.at[1],
        device_id=(lax.rem(me + n - 1, n),),
        device_id_type=MESH,
    )
    has_next = me < n - 1
    has_prior = me > 0

    @pl.when(has_next)
    def _():
        to_next.start()

    @pl.when(has_prior)
    def _():
        to_prior.start()

    @pl.when(jnp.logical_not(has_prior))
    def _():
        xext[0:HALO] = jnp.zeros((HALO, leaf, rhs), BF16)

    @pl.when(jnp.logical_not(has_next))
    def _():
        xext[HALO + leaves :] = jnp.zeros((HALO, leaf, rhs), BF16)

    for pair in range(leaves // 2):
        rows = []
        for g in (2 * pair, 2 * pair + 1):
            for odd in range(2):
                rows.append(coef_f[g, pl.ds(odd, half, stride=2), :])
        tile = jnp.concatenate(rows, axis=0)
        coef_t[:, pair * 2 * rank : (pair + 1) * 2 * rank] = tile.T.astype(BF16)

    keys[...] = jnp.full(keys.shape, -1, jnp.int32)
    for b in range(rows_v.shape[0]):
        keys[b : b + 1, :] = cols_v[b : b + 1, :] * leaves + rows_v[b : b + 1, :]
    b = rows_v.shape[0]
    keys[b : b + 1, 0:nb] = nrows_v[...] + rlast
    keys[b + 1 : b + 2, 0:nb] = ncols_v[...] + klast
    keys[b + 2 : b + 3, 0:n] = send_v[...] + qlast
    chains(keys, prev_v, last_v, parts, id_parts)
    prev_load = pltpu.make_async_copy(prev_v, prev_s, load_sem.at[4])
    last_load = pltpu.make_async_copy(last_v, last_s, load_sem.at[5])
    prev_load.start()
    last_load.start()
    prev_load.wait()
    last_load.wait()

    load_s.wait()

    chained[cb] = jnp.zeros((half, 2 * rank), F32)
    plain[cb] = jnp.zeros((half, 2 * rank), BF16)
    rolled[cb] = jnp.zeros((half, 2 * rank), BF16)

    def spread(t, carry):
        for j in range(half):
            piece = blocks[pl.ds(pl.multiple_of(t * 16, 16), 16), j * 2 * rank : (j + 1) * 2 * rank]
            raw[pl.ds(j, 16, stride=half), :] = piece.astype(F32)
        for s in range(16):
            k = t * 16 + s
            value = raw[s * half : (s + 1) * half, :] + chained[at(prev_s, k)]
            chained[k] = value
            plain[k] = value.astype(BF16)
            rolled[k] = pltpu.roll(value, rank, 1).astype(BF16)
        return carry

    lax.fori_loop(0, cb // 16, spread, 0, unroll=1)

    groups = n // 4
    my_group = me // 4
    part = min(16, n // 2)

    def back_copy(q):
        return pltpu.make_async_remote_copy(
            src_ref=sums.at[q],
            dst_ref=back.at[me],
            send_sem=send2,
            recv_sem=recv2.at[me // part],
            device_id=(q,),
            device_id_type=MESH,
        )

    def mirror(i, carry):
        g = lax.rem(my_group + i * 5, groups)
        rows = []
        for r in range(leaves):
            upper, lower = [], []
            for pair in range(2):
                k0 = last_s[g // 4, g % 4 * 4 * leaves + 2 * pair * leaves + r]
                k1 = last_s[g // 4, g % 4 * 4 * leaves + (2 * pair + 1) * leaves + r]
                upper.append(jnp.where(low_half, plain[k0], rolled[k1]))
                lower.append(jnp.where(low_half, rolled[k0], plain[k1]))
            rows.append(jnp.concatenate(upper, axis=1))
            rows.append(jnp.concatenate(lower, axis=1))
        tile = jnp.concatenate(rows, axis=0)
        dense[g] = tile
        product = jnp.dot(coef_t[...], tile, preferred_element_type=F32)
        for pair in range(2):
            part = product[:, pair * 2 * rank : (pair + 1) * 2 * rank]
            top, bottom = part[:rank], part[rank:]
            turned = pltpu.roll(jnp.where(low, bottom, top), rank, 1)
            sums[g * 4 + 2 * pair] = jnp.where(low, top, turned).astype(BF16)
            sums[g * 4 + 2 * pair + 1] = jnp.where(low, turned, bottom).astype(BF16)
        for s in range(4):
            q = g * 4 + s

            @pl.when(q != me)
            def _():
                back_copy(q).start()

            @pl.when(q == me)
            def _():
                back[me] = sums[me]

        return carry

    lax.fori_loop(0, groups, mirror, 0, unroll=2)

    for g in range(leaves):
        x_t[g] = xext[HALO + g].astype(F32).T.astype(BF16)
        basis_t[g] = basis[g].astype(F32).T.astype(BF16)

    @pl.when(has_prior)
    def _():
        to_next.wait_recv()

    @pl.when(has_next)
    def _():
        to_prior.wait_recv()

    load_n.wait()
    work[nb] = jnp.zeros((leaf, rhs), F32)

    def near_rows(k, carry):
        y = jnp.dot(near[k], xext[ncols_ref[k]], preferred_element_type=F32)
        work[k] = y + work[at(prev_s, rprev + k)]
        return carry

    lax.fori_loop(0, nb, near_rows, 0, unroll=8)
    for g in range(leaves):
        near_sum[g] = work[at(last_s, rlast + g)]

    def near_cols(k, carry):
        y = jnp.dot(x_t[nrows_ref[k]], near[k], preferred_element_type=F32)
        before = work[at(prev_s, kprev + k)]
        for h in range(2):
            rows = slice(h * rhs, (h + 1) * rhs)
            work[k, rows, :] = y[:, rows] + before[rows]
        return carry

    lax.fori_loop(0, nb, near_cols, 0, unroll=8)

    def spread_of(c):
        return work[at(last_s, klast + c)]

    for h in range(HALO):
        rim_out[0, h] = spread_of(h).astype(BF16)
        rim_out[1, h] = spread_of(HALO + leaves + h).astype(BF16)
    rim_prior = pltpu.make_async_remote_copy(
        src_ref=rim_out.at[0],
        dst_ref=rim_in.at[0],
        send_sem=rsend.at[0],
        recv_sem=rrecv.at[0],
        device_id=(lax.rem(me + n - 1, n),),
        device_id_type=MESH,
    )
    rim_next = pltpu.make_async_remote_copy(
        src_ref=rim_out.at[1],
        dst_ref=rim_in.at[1],
        send_sem=rsend.at[1],
        recv_sem=rrecv.at[1],
        device_id=(lax.rem(me + 1, n),),
        device_id_type=MESH,
    )

    @pl.when(has_prior)
    def _():
        rim_prior.start()

    @pl.when(has_next)
    def _():
        rim_next.start()

    def add_turned(g, y):
        for h in range(2):
            rows = slice(h * rhs, (h + 1) * rhs)
            near_sum[g, rows, :] += y[rows].T

    for g in range(leaves):
        add_turned(g, spread_of(HALO + g))

    others = pl.ds(0, (n - 1) * rank)
    all_forward = pltpu.make_async_remote_copy(
        src_ref=received.at[others],
        dst_ref=received.at[others],
        send_sem=send1,
        recv_sem=recv1,
        device_id=(lax.rem(me + 1, n),),
        device_id_type=MESH,
    )
    all_forward.wait_recv()
    all_forward.wait_send()
    total[...] = jnp.zeros_like(total)
    step = min(4, groups)

    def forward(i, carry):
        acc = total[...]
        for s in range(step):
            g = i * step + s
            c = received[pl.ds(pl.multiple_of(g * 4 * rank, 4 * rank), 4 * rank), :]
            acc = acc + jnp.dot(dense[g], c, preferred_element_type=F32)
        total[...] = acc
        return carry

    lax.fori_loop(0, groups // step, forward, 0)

    @pl.when(has_next)
    def _():
        rim_prior.wait_recv()
        for h in range(HALO):
            add_turned(leaves - HALO + h, rim_in[0, h].astype(F32))

    @pl.when(has_prior)
    def _():
        rim_next.wait_recv()
        for h in range(HALO):
            add_turned(h, rim_in[1, h].astype(F32))

    back_sum[n] = jnp.zeros((rank, rhs), F32)

    def arrived(i, count):
        return pltpu.make_async_remote_copy(
            src_ref=back.at[pl.ds(0, count)],
            dst_ref=back.at[pl.ds(0, count)],
            send_sem=send2,
            recv_sem=recv2.at[i],
            device_id=(lax.rem(me + 1, n),),
            device_id_type=MESH,
        )

    def returned(i, carry):
        @pl.when(me // part == i)
        def _():
            arrived(i, part - 1).wait_recv()

        @pl.when(me // part != i)
        def _():
            arrived(i, part).wait_recv()

        for s in range(part):
            q = i * part + s
            back_sum[q] = back[q].astype(F32) + back_sum[at(prev_s, qprev + q)]
        return carry

    lax.fori_loop(0, n // part, returned, 0)
    arrived(0, n - 1).wait_send()

    def store(g):
        return pltpu.make_async_copy(out.at[g], out_hbm.at[g], load_sem.at[6 + g])

    for g in range(leaves):
        y = back_sum[at(last_s, qlast + g)]
        turned = jnp.concatenate([y, pltpu.roll(y, rank, 1)], axis=0).T
        far_f[g, pl.ds(0, half, stride=2), :] = total[g * rank : g * rank + half, :]
        far_f[g, pl.ds(1, half, stride=2), :] = total[g * rank + half : (g + 1) * rank, :]
        far = (far_f[g] + turned[:rank]).astype(BF16)
        down = jnp.dot(basis_t[g], far, preferred_element_type=F32)
        out[g] = (down + near_sum[g]).astype(BF16)
        store(g).start()

    @pl.when(has_next)
    def _():
        to_next.wait_send()
        rim_next.wait_send()

    @pl.when(has_prior)
    def _():
        to_prior.wait_send()
        rim_prior.wait_send()

    for g in range(leaves):
        store(g).wait()


def per_device(
    features,
    basis_t,
    send_list,
    couple_rows,
    couple_cols,
    couple_blocks,
    near_rows,
    near_cols,
    near_blocks,
):
    n = lax.axis_size("clus")
    leaves, rank, leaf = basis_t.shape
    rhs = features.shape[1]
    cb, nb = couple_blocks.shape[0], near_blocks.shape[0]
    send = send_list.reshape(-1)
    base = -(-n * leaves // 128) * 128
    key_rows = cb // 128 + 3
    half = rank // 2
    wide = leaves + 2 * HALO
    dma = pltpu.SemaphoreType.DMA
    smem = pl.BlockSpec(memory_space=pltpu.SMEM)
    anywhere = pl.BlockSpec(memory_space=pl.ANY)
    return pl.pallas_call(
        functools.partial(kernel, n, leaves, rank, leaf, rhs, cb, nb),
        out_shape=jax.ShapeDtypeStruct((leaves, leaf, rhs), BF16),
        in_specs=[smem] * 3 + [pl.BlockSpec(memory_space=pltpu.VMEM)] * 5 + [anywhere] * 4,
        out_specs=anywhere,
        scratch_shapes=[
            pltpu.VMEM((wide, leaf, rhs), BF16),
            pltpu.VMEM((leaves, rank, leaf), BF16),
            pltpu.VMEM((leaves, leaf, rank), BF16),
            pltpu.VMEM(couple_blocks.shape, BF16),
            pltpu.VMEM(near_blocks.shape, BF16),
            pltpu.VMEM((leaves, rank, rhs), BF16),
            pltpu.VMEM((leaves, rank, rhs), F32),
            pltpu.VMEM((rhs, leaves * rank), BF16),
            pltpu.VMEM((leaves, rhs, leaf), BF16),
            pltpu.VMEM((n, rank, rhs), BF16),
            pltpu.VMEM((n * rank, rhs), BF16),
            pltpu.VMEM((cb + 1, half, 2 * rank), BF16),
            pltpu.VMEM((cb + 1, half, 2 * rank), BF16),
            pltpu.VMEM((n // 4, leaves * rank, 4 * rank), BF16),
            pltpu.VMEM((n, rank, rhs), BF16),
            pltpu.VMEM((n, rank, rhs), BF16),
            pltpu.VMEM((leaves * rank, rhs), F32),
            pltpu.VMEM((16 * half, 2 * rank), F32),
            pltpu.VMEM((cb + 1, half, 2 * rank), F32),
            pltpu.VMEM((nb + 1, leaf, rhs), F32),
            pltpu.VMEM((n + 1, rank, rhs), F32),
            pltpu.VMEM((leaves, leaf, rhs), F32),
            pltpu.VMEM((2, HALO, leaf, rhs), BF16),
            pltpu.VMEM((2, HALO, leaf, rhs), BF16),
            pltpu.VMEM((leaves, leaf, rhs), BF16),
            pltpu.VMEM((leaves, rank, rhs), F32),
            pltpu.VMEM((key_rows, 128), jnp.int32),
            pltpu.VMEM((key_rows, 128), jnp.int32),
            pltpu.VMEM((base // 128 + 1, 128), jnp.int32),
            pltpu.SMEM((key_rows, 128), jnp.int32),
            pltpu.SMEM((base // 128 + 1, 128), jnp.int32),
            dma((6 + leaves,)),
            dma,
            dma,
            dma,
            dma((n // min(16, n // 2),)),
            dma((2,)),
            dma((2,)),
            dma((2,)),
            dma((2,)),
        ],
        compiler_params=pltpu.CompilerParams(
            collective_id=0, has_side_effects=True, vmem_limit_bytes=60 * 1024 * 1024
        ),
    )(
        send,
        near_rows,
        near_cols,
        couple_rows.reshape(-1, 128),
        couple_cols.reshape(-1, 128),
        near_rows.reshape(1, nb),
        near_cols.reshape(1, nb),
        send.reshape(1, n),
        features.reshape(leaves, leaf, rhs),
        basis_t,
        couple_blocks,
        near_blocks,
    ).reshape(features.shape)


def solution(mesh):
    placed = (
        P("clus", None),
        P("clus", None, None),
        P("clus", None, None),
        P("clus"),
        P("clus"),
        P("clus", None),
        P("clus"),
        P("clus"),
        P("clus", None, None),
    )
    return jax.shard_map(
        per_device, mesh=mesh, in_specs=placed, out_specs=P("clus", None), check_vma=False
    )
```

```python
import functools
import random

import jax
import jax.numpy as jnp
from jax import lax
from jax.experimental import pallas as pl
from jax.experimental.pallas import tpu as pltpu
from jax.sharding import PartitionSpec as P

HALO = 2
MESH = pl.DeviceIdType.MESH
F32 = jnp.float32
BF16 = jnp.bfloat16


def chains(keys_ref, prev_ref, last_ref, parts, id_parts):
    blocks = keys_ref.shape[0]
    row = lax.broadcasted_iota(jnp.int32, (128, 128), 0)
    col = lax.broadcasted_iota(jnp.int32, (128, 128), 1)
    down = [jnp.broadcast_to(keys_ref[b : b + 1, :], (128, 128)).T for b in range(blocks)]
    lane = lax.broadcasted_iota(jnp.int32, (1, 128), 1)

    def settle(found, place, bounds):
        start, length = jnp.zeros_like(place), jnp.zeros_like(place)
        for first, (at, size) in bounds:
            start = jnp.where(place >= first, at, start)
            length = jnp.where(place >= first, size, length)
        return jnp.where(found < 0, length, jnp.clip(found - start, 0, length))

    for b in range(blocks):
        key = keys_ref[b : b + 1, :]
        best = jnp.full((128, 128), -1, jnp.int32)
        for other in range(b + 1):
            hit = down[other] == key
            if other == b:
                hit = hit & (row < col)
            best = jnp.where(hit, row + other * 128, best)
        found = jnp.max(best, axis=0, keepdims=True)
        prev_ref[b : b + 1, :] = settle(found, lane + b * 128, [(start, (start, size)) for start, size in parts])
    for b in range(last_ref.shape[0]):
        best = jnp.full((128, 128), -1, jnp.int32)
        for other in range(blocks):
            best = jnp.where(down[other] == lane + b * 128, row + other * 128, best)
        found = jnp.max(best, axis=0, keepdims=True)
        last_ref[b : b + 1, :] = settle(found, lane + b * 128, [(first, parts[part]) for first, part in id_parts])


def near_first(n):
    steps = [(o // 32, o // 8 % 4, o // 2 % 4, o % 2) for o in range(1, n)]
    random.Random(0).shuffle(steps)
    steps.sort(key=lambda o: sum(min(v, 4 - v) for v in o[:3]))
    return steps


def kernel(
    n,
    leaves,
    rank,
    leaf,
    rhs,
    cb,
    nb,
    send_ref,
    nrows_ref,
    ncols_ref,
    rows_v,
    cols_v,
    nrows_v,
    ncols_v,
    send_v,
    x_hbm,
    basis_hbm,
    blocks_hbm,
    near_hbm,
    out_hbm,
    xext,
    basis,
    basis_t,
    blocks,
    near,
    coef,
    coef_f,
    coef_t,
    x_t,
    outgoing,
    received,
    plain,
    rolled,
    dense,
    sums,
    back,
    total,
    raw,
    chained,
    work,
    back_sum,
    near_sum,
    rim_out,
    rim_in,
    out,
    far_f,
    keys,
    prev_v,
    last_v,
    prev_s,
    last_s,
    load_sem,
    send1,
    recv1,
    send2,
    recv2,
    hsend,
    hrecv,
    rsend,
    rrecv,
):
    me = lax.axis_index("clus")
    base = last_v.shape[0] * 128 - 128
    rprev = rows_v.shape[0] * 128
    kprev, qprev = rprev + 128, rprev + 256
    rlast, klast, qlast = base, base + leaves, base + 2 * leaves + 2 * HALO
    parts = [(0, cb), (rprev, nb), (kprev, nb), (qprev, n)]
    id_parts = [(0, 0), (rlast, 1), (klast, 2), (qlast, 3)]

    def at(ref, i):
        return ref[i // 128, i % 128]

    def target(q):
        return send_ref[q]

    half = rank // 2
    lane = lax.broadcasted_iota(jnp.int32, (rank, 2 * rank), 1)
    low = lane < rank
    low_half = lax.broadcasted_iota(jnp.int32, (half, 2 * rank), 1) < rank

    barrier = pltpu.get_barrier_semaphore()

    load_x = pltpu.make_async_copy(x_hbm, xext.at[pl.ds(HALO, leaves)], load_sem.at[0])
    load_b = pltpu.make_async_copy(basis_hbm, basis, load_sem.at[1])
    load_s = pltpu.make_async_copy(blocks_hbm, blocks, load_sem.at[2])
    load_n = pltpu.make_async_copy(near_hbm, near, load_sem.at[3])
    load_x.start()
    load_b.start()

    def greet(i, carry):
        q = lax.rem(me + i, n)
        pl.semaphore_signal(barrier, inc=1, device_id=(q,), device_id_type=MESH)
        return carry

    lax.fori_loop(1, n, greet, 0)

    load_x.wait()
    load_b.wait()
    load_s.start()

    def coefficients(g, carry):
        c = jnp.dot(basis[g], xext[HALO + g], preferred_element_type=F32).astype(BF16)
        coef[g] = c
        coef_f[g] = c.astype(F32)
        return carry

    lax.fori_loop(0, leaves, coefficients, 0, unroll=leaves)
    load_n.start()

    pl.semaphore_wait(barrier, n - 1)

    def forward_copy(q):
        return pltpu.make_async_remote_copy(
            src_ref=outgoing.at[q],
            dst_ref=received.at[pl.ds(pl.multiple_of(me * rank, rank), rank)],
            send_sem=send1,
            recv_sem=recv1,
            device_id=(q,),
            device_id_type=MESH,
        )

    def peer(step):
        x, z, y, core = me // 32, me // 8 % 4, me // 2 % 4, me % 2
        dx, dz, dy, dc = step
        return (((x + dx) % (n // 32) * 4 + (z + dz) % 4) * 4 + (y + dy) % 4) * 2 + (core + dc) % 2

    for step in near_first(n):
        q = peer(step)
        outgoing[q] = coef[target(q)]
        forward_copy(q).start()
    received[pl.ds(pl.multiple_of(me * rank, rank), rank), :] = coef[target(me)]

    to_next = pltpu.make_async_remote_copy(
        src_ref=xext.at[pl.ds(leaves, HALO)],
        dst_ref=xext.at[pl.ds(0, HALO)],
        send_sem=hsend.at[0],
        recv_sem=hrecv.at[0],
        device_id=(lax.rem(me + 1, n),),
        device_id_type=MESH,
    )
    to_prior = pltpu.make_async_remote_copy(
        src_ref=xext.at[pl.ds(HALO, HALO)],
        dst_ref=xext.at[pl.ds(HALO + leaves, HALO)],
        send_sem=hsend.at[1],
        recv_sem=hrecv.at[1],
        device_id=(lax.rem(me + n - 1, n),),
        device_id_type=MESH,
    )
    has_next = me < n - 1
    has_prior = me > 0

    @pl.when(has_next)
    def _():
        to_next.start()

    @pl.when(has_prior)
    def _():
        to_prior.start()

    @pl.when(jnp.logical_not(has_prior))
    def _():
        xext[0:HALO] = jnp.zeros((HALO, leaf, rhs), BF16)

    @pl.when(jnp.logical_not(has_next))
    def _():
        xext[HALO + leaves :] = jnp.zeros((HALO, leaf, rhs), BF16)

    for pair in range(leaves // 2):
        rows = []
        for g in (2 * pair, 2 * pair + 1):
            for odd in range(2):
                rows.append(coef_f[g, pl.ds(odd, half, stride=2), :])
        tile = jnp.concatenate(rows, axis=0)
        coef_t[:, pair * 2 * rank : (pair + 1) * 2 * rank] = tile.T.astype(BF16)

    keys[...] = jnp.full(keys.shape, -1, jnp.int32)
    for b in range(rows_v.shape[0]):
        keys[b : b + 1, :] = cols_v[b : b + 1, :] * leaves + rows_v[b : b + 1, :]
    b = rows_v.shape[0]
    keys[b : b + 1, 0:nb] = nrows_v[...] + rlast
    keys[b + 1 : b + 2, 0:nb] = ncols_v[...] + klast
    keys[b + 2 : b + 3, 0:n] = send_v[...] + qlast
    chains(keys, prev_v, last_v, parts, id_parts)
    prev_load = pltpu.make_async_copy(prev_v, prev_s, load_sem.at[4])
    last_load = pltpu.make_async_copy(last_v, last_s, load_sem.at[5])
    prev_load.start()
    last_load.start()
    prev_load.wait()
    last_load.wait()

    load_s.wait()

    chained[cb] = jnp.zeros((half, 2 * rank), F32)
    plain[cb] = jnp.zeros((half, 2 * rank), BF16)
    rolled[cb] = jnp.zeros((half, 2 * rank), BF16)

    def spread(t, carry):
        for j in range(half):
            piece = blocks[pl.ds(pl.multiple_of(t * 16, 16), 16), j * 2 * rank : (j + 1) * 2 * rank]
            raw[pl.ds(j, 16, stride=half), :] = piece.astype(F32)
        for s in range(16):
            k = t * 16 + s
            value = raw[s * half : (s + 1) * half, :] + chained[at(prev_s, k)]
            chained[k] = value
            plain[k] = value.astype(BF16)
            rolled[k] = pltpu.roll(value, rank, 1).astype(BF16)
        return carry

    lax.fori_loop(0, cb // 16, spread, 0, unroll=1)

    groups = n // 4
    my_group = me // 4
    part = min(16, n // 2)

    def back_copy(q):
        return pltpu.make_async_remote_copy(
            src_ref=sums.at[q],
            dst_ref=back.at[me],
            send_sem=send2,
            recv_sem=recv2.at[me // part],
            device_id=(q,),
            device_id_type=MESH,
        )

    def mirror(i, carry):
        g = lax.rem(my_group + i * 5, groups)
        rows = []
        for r in range(leaves):
            upper, lower = [], []
            for pair in range(2):
                k0 = last_s[g // 4, g % 4 * 4 * leaves + 2 * pair * leaves + r]
                k1 = last_s[g // 4, g % 4 * 4 * leaves + (2 * pair + 1) * leaves + r]
                upper.append(jnp.where(low_half, plain[k0], rolled[k1]))
                lower.append(jnp.where(low_half, rolled[k0], plain[k1]))
            rows.append(jnp.concatenate(upper, axis=1))
            rows.append(jnp.concatenate(lower, axis=1))
        tile = jnp.concatenate(rows, axis=0)
        dense[g] = tile
        product = jnp.dot(coef_t[...], tile, preferred_element_type=F32)
        for pair in range(2):
            part = product[:, pair * 2 * rank : (pair + 1) * 2 * rank]
            top, bottom = part[:rank], part[rank:]
            turned = pltpu.roll(jnp.where(low, bottom, top), rank, 1)
            sums[g * 4 + 2 * pair] = jnp.where(low, top, turned).astype(BF16)
            sums[g * 4 + 2 * pair + 1] = jnp.where(low, turned, bottom).astype(BF16)
        for s in range(4):
            q = g * 4 + s

            @pl.when(q != me)
            def _():
                back_copy(q).start()

            @pl.when(q == me)
            def _():
                back[me] = sums[me]

        return carry

    lax.fori_loop(0, groups, mirror, 0, unroll=2)

    for g in range(leaves):
        x_t[g] = xext[HALO + g].astype(F32).T.astype(BF16)
        basis_t[g] = basis[g].astype(F32).T.astype(BF16)

    @pl.when(has_prior)
    def _():
        to_next.wait_recv()

    @pl.when(has_next)
    def _():
        to_prior.wait_recv()

    load_n.wait()
    work[nb] = jnp.zeros((leaf, rhs), F32)

    def near_rows(k, carry):
        y = jnp.dot(near[k], xext[ncols_ref[k]], preferred_element_type=F32)
        work[k] = y + work[at(prev_s, rprev + k)]
        return carry

    lax.fori_loop(0, nb, near_rows, 0, unroll=8)
    for g in range(leaves):
        near_sum[g] = work[at(last_s, rlast + g)]

    def near_cols(k, carry):
        y = jnp.dot(x_t[nrows_ref[k]], near[k], preferred_element_type=F32)
        before = work[at(prev_s, kprev + k)]
        for h in range(2):
            rows = slice(h * rhs, (h + 1) * rhs)
            work[k, rows, :] = y[:, rows] + before[rows]
        return carry

    lax.fori_loop(0, nb, near_cols, 0, unroll=8)

    def spread_of(c):
        return work[at(last_s, klast + c)]

    for h in range(HALO):
        rim_out[0, h] = spread_of(h).astype(BF16)
        rim_out[1, h] = spread_of(HALO + leaves + h).astype(BF16)
    rim_prior = pltpu.make_async_remote_copy(
        src_ref=rim_out.at[0],
        dst_ref=rim_in.at[0],
        send_sem=rsend.at[0],
        recv_sem=rrecv.at[0],
        device_id=(lax.rem(me + n - 1, n),),
        device_id_type=MESH,
    )
    rim_next = pltpu.make_async_remote_copy(
        src_ref=rim_out.at[1],
        dst_ref=rim_in.at[1],
        send_sem=rsend.at[1],
        recv_sem=rrecv.at[1],
        device_id=(lax.rem(me + 1, n),),
        device_id_type=MESH,
    )

    @pl.when(has_prior)
    def _():
        rim_prior.start()

    @pl.when(has_next)
    def _():
        rim_next.start()

    def add_turned(g, y):
        for h in range(2):
            rows = slice(h * rhs, (h + 1) * rhs)
            near_sum[g, rows, :] += y[rows].T

    for g in range(leaves):
        add_turned(g, spread_of(HALO + g))

    others = pl.ds(0, (n - 1) * rank)
    all_forward = pltpu.make_async_remote_copy(
        src_ref=received.at[others],
        dst_ref=received.at[others],
        send_sem=send1,
        recv_sem=recv1,
        device_id=(lax.rem(me + 1, n),),
        device_id_type=MESH,
    )
    all_forward.wait_recv()
    all_forward.wait_send()
    total[...] = jnp.zeros_like(total)
    step = min(4, groups)

    def forward(i, carry):
        acc = total[...]
        for s in range(step):
            g = i * step + s
            c = received[pl.ds(pl.multiple_of(g * 4 * rank, 4 * rank), 4 * rank), :]
            acc = acc + jnp.dot(dense[g], c, preferred_element_type=F32)
        total[...] = acc
        return carry

    lax.fori_loop(0, groups // step, forward, 0)
    for g in range(leaves):
        far_f[g, pl.ds(0, half, stride=2), :] = total[g * rank : g * rank + half, :]
        far_f[g, pl.ds(1, half, stride=2), :] = total[g * rank + half : (g + 1) * rank, :]

    @pl.when(has_next)
    def _():
        rim_prior.wait_recv()
        for h in range(HALO):
            add_turned(leaves - HALO + h, rim_in[0, h].astype(F32))

    @pl.when(has_prior)
    def _():
        rim_next.wait_recv()
        for h in range(HALO):
            add_turned(h, rim_in[1, h].astype(F32))

    back_sum[n] = jnp.zeros((rank, rhs), F32)

    def arrived(i, count):
        return pltpu.make_async_remote_copy(
            src_ref=back.at[pl.ds(0, count)],
            dst_ref=back.at[pl.ds(0, count)],
            send_sem=send2,
            recv_sem=recv2.at[i],
            device_id=(lax.rem(me + 1, n),),
            device_id_type=MESH,
        )

    def returned(i, carry):
        @pl.when(me // part == i)
        def _():
            arrived(i, part - 1).wait_recv()

        @pl.when(me // part != i)
        def _():
            arrived(i, part).wait_recv()

        for s in range(part):
            q = i * part + s
            back_sum[q] = back[q].astype(F32) + back_sum[at(prev_s, qprev + q)]
        return carry

    lax.fori_loop(0, n // part, returned, 0)

    def store(g):
        return pltpu.make_async_copy(out.at[g], out_hbm.at[g], load_sem.at[6 + g])

    for g in range(leaves):
        y = back_sum[at(last_s, qlast + g)]
        turned = jnp.concatenate([y, pltpu.roll(y, rank, 1)], axis=0).T
        far = (far_f[g] + turned[:rank]).astype(BF16)
        down = jnp.dot(basis_t[g], far, preferred_element_type=F32)
        out[g] = (down + near_sum[g]).astype(BF16)
        store(g).start()

    @pl.when(has_next)
    def _():
        to_next.wait_send()
        rim_next.wait_send()

    @pl.when(has_prior)
    def _():
        to_prior.wait_send()
        rim_prior.wait_send()

    arrived(0, n - 1).wait_send()
    for g in range(leaves):
        store(g).wait()


def per_device(
    features,
    basis_t,
    send_list,
    couple_rows,
    couple_cols,
    couple_blocks,
    near_rows,
    near_cols,
    near_blocks,
):
    n = lax.axis_size("clus")
    leaves, rank, leaf = basis_t.shape
    rhs = features.shape[1]
    cb, nb = couple_blocks.shape[0], near_blocks.shape[0]
    send = send_list.reshape(-1)
    base = -(-n * leaves // 128) * 128
    key_rows = cb // 128 + 3
    half = rank // 2
    wide = leaves + 2 * HALO
    dma = pltpu.SemaphoreType.DMA
    smem = pl.BlockSpec(memory_space=pltpu.SMEM)
    anywhere = pl.BlockSpec(memory_space=pl.ANY)
    return pl.pallas_call(
        functools.partial(kernel, n, leaves, rank, leaf, rhs, cb, nb),
        out_shape=jax.ShapeDtypeStruct((leaves, leaf, rhs), BF16),
        in_specs=[smem] * 3 + [pl.BlockSpec(memory_space=pltpu.VMEM)] * 5 + [anywhere] * 4,
        out_specs=anywhere,
        scratch_shapes=[
            pltpu.VMEM((wide, leaf, rhs), BF16),
            pltpu.VMEM((leaves, rank, leaf), BF16),
            pltpu.VMEM((leaves, leaf, rank), BF16),
            pltpu.VMEM(couple_blocks.shape, BF16),
            pltpu.VMEM(near_blocks.shape, BF16),
            pltpu.VMEM((leaves, rank, rhs), BF16),
            pltpu.VMEM((leaves, rank, rhs), F32),
            pltpu.VMEM((rhs, leaves * rank), BF16),
            pltpu.VMEM((leaves, rhs, leaf), BF16),
            pltpu.VMEM((n, rank, rhs), BF16),
            pltpu.VMEM((n * rank, rhs), BF16),
            pltpu.VMEM((cb + 1, half, 2 * rank), BF16),
            pltpu.VMEM((cb + 1, half, 2 * rank), BF16),
            pltpu.VMEM((n // 4, leaves * rank, 4 * rank), BF16),
            pltpu.VMEM((n, rank, rhs), BF16),
            pltpu.VMEM((n, rank, rhs), BF16),
            pltpu.VMEM((leaves * rank, rhs), F32),
            pltpu.VMEM((16 * half, 2 * rank), F32),
            pltpu.VMEM((cb + 1, half, 2 * rank), F32),
            pltpu.VMEM((nb + 1, leaf, rhs), F32),
            pltpu.VMEM((n + 1, rank, rhs), F32),
            pltpu.VMEM((leaves, leaf, rhs), F32),
            pltpu.VMEM((2, HALO, leaf, rhs), BF16),
            pltpu.VMEM((2, HALO, leaf, rhs), BF16),
            pltpu.VMEM((leaves, leaf, rhs), BF16),
            pltpu.VMEM((leaves, rank, rhs), F32),
            pltpu.VMEM((key_rows, 128), jnp.int32),
            pltpu.VMEM((key_rows, 128), jnp.int32),
            pltpu.VMEM((base // 128 + 1, 128), jnp.int32),
            pltpu.SMEM((key_rows, 128), jnp.int32),
            pltpu.SMEM((base // 128 + 1, 128), jnp.int32),
            dma((6 + leaves,)),
            dma,
            dma,
            dma,
            dma((n // min(16, n // 2),)),
            dma((2,)),
            dma((2,)),
            dma((2,)),
            dma((2,)),
        ],
        compiler_params=pltpu.CompilerParams(
            collective_id=0, has_side_effects=True, vmem_limit_bytes=60 * 1024 * 1024
        ),
    )(
        send,
        near_rows,
        near_cols,
        couple_rows.reshape(-1, 128),
        couple_cols.reshape(-1, 128),
        near_rows.reshape(1, nb),
        near_cols.reshape(1, nb),
        send.reshape(1, n),
        features.reshape(leaves, leaf, rhs),
        basis_t,
        couple_blocks,
        near_blocks,
    ).reshape(features.shape)


def solution(mesh):
    placed = (
        P("clus", None),
        P("clus", None, None),
        P("clus", None, None),
        P("clus"),
        P("clus"),
        P("clus", None),
        P("clus"),
        P("clus"),
        P("clus", None, None),
    )
    return jax.shard_map(
        per_device, mesh=mesh, in_specs=placed, out_specs=P("clus", None), check_vma=False
    )
```

```python
import functools
import random

import jax
import jax.numpy as jnp
from jax import lax
from jax.experimental import pallas as pl
from jax.experimental.pallas import tpu as pltpu
from jax.sharding import PartitionSpec as P

HALO = 2
MESH = pl.DeviceIdType.MESH
F32 = jnp.float32
BF16 = jnp.bfloat16


def chains(keys_ref, prev_ref, last_ref, parts, id_parts):
    blocks = keys_ref.shape[0]
    row = lax.broadcasted_iota(jnp.int32, (128, 128), 0)
    col = lax.broadcasted_iota(jnp.int32, (128, 128), 1)
    down = [jnp.broadcast_to(keys_ref[b : b + 1, :], (128, 128)).T for b in range(blocks)]
    lane = lax.broadcasted_iota(jnp.int32, (1, 128), 1)

    def settle(found, place, bounds):
        start, length = jnp.zeros_like(place), jnp.zeros_like(place)
        for first, (at, size) in bounds:
            start = jnp.where(place >= first, at, start)
            length = jnp.where(place >= first, size, length)
        return jnp.where(found < 0, length, jnp.clip(found - start, 0, length))

    for b in range(blocks):
        key = keys_ref[b : b + 1, :]
        best = jnp.full((128, 128), -1, jnp.int32)
        for other in range(b + 1):
            hit = down[other] == key
            if other == b:
                hit = hit & (row < col)
            best = jnp.where(hit, row + other * 128, best)
        found = jnp.max(best, axis=0, keepdims=True)
        prev_ref[b : b + 1, :] = settle(found, lane + b * 128, [(start, (start, size)) for start, size in parts])
    for b in range(last_ref.shape[0]):
        best = jnp.full((128, 128), -1, jnp.int32)
        for other in range(blocks):
            best = jnp.where(down[other] == lane + b * 128, row + other * 128, best)
        found = jnp.max(best, axis=0, keepdims=True)
        last_ref[b : b + 1, :] = settle(found, lane + b * 128, [(first, parts[part]) for first, part in id_parts])


def near_first(n):
    steps = [(o // 32, o // 8 % 4, o // 2 % 4, o % 2) for o in range(1, n)]
    random.Random(0).shuffle(steps)
    steps.sort(key=lambda o: sum(min(v, 4 - v) for v in o[:3]))
    return steps


def kernel(
    n,
    leaves,
    rank,
    leaf,
    rhs,
    cb,
    nb,
    send_ref,
    nrows_ref,
    ncols_ref,
    rows_v,
    cols_v,
    nrows_v,
    ncols_v,
    send_v,
    x_hbm,
    basis_hbm,
    blocks_hbm,
    near_hbm,
    out_hbm,
    xext,
    basis,
    basis_t,
    blocks,
    near,
    coef,
    coef_f,
    coef_t,
    x_t,
    outgoing,
    received,
    plain,
    rolled,
    dense,
    sums,
    back,
    total,
    raw,
    chained,
    work,
    back_sum,
    near_sum,
    rim_out,
    rim_in,
    out,
    far_f,
    keys,
    prev_v,
    last_v,
    prev_s,
    last_s,
    load_sem,
    send1,
    recv1,
    send2,
    recv2,
    hsend,
    hrecv,
    rsend,
    rrecv,
):
    me = lax.axis_index("clus")
    base = last_v.shape[0] * 128 - 128
    rprev = rows_v.shape[0] * 128
    kprev, qprev = rprev + 128, rprev + 256
    rlast, klast, qlast = base, base + leaves, base + 2 * leaves + 2 * HALO
    parts = [(0, cb), (rprev, nb), (kprev, nb), (qprev, n)]
    id_parts = [(0, 0), (rlast, 1), (klast, 2), (qlast, 3)]

    def at(ref, i):
        return ref[i // 128, i % 128]

    def target(q):
        return send_ref[q]

    half = rank // 2
    lane = lax.broadcasted_iota(jnp.int32, (rank, 2 * rank), 1)
    low = lane < rank
    low_half = lax.broadcasted_iota(jnp.int32, (half, 2 * rank), 1) < rank

    barrier = pltpu.get_barrier_semaphore()

    load_x = pltpu.make_async_copy(x_hbm, xext.at[pl.ds(HALO, leaves)], load_sem.at[0])
    load_b = pltpu.make_async_copy(basis_hbm, basis, load_sem.at[1])
    load_s = pltpu.make_async_copy(blocks_hbm, blocks, load_sem.at[2])
    load_n = pltpu.make_async_copy(near_hbm, near, load_sem.at[3])
    load_x.start()
    load_b.start()

    def greet(i, carry):
        q = lax.rem(me + i, n)
        pl.semaphore_signal(barrier, inc=1, device_id=(q,), device_id_type=MESH)
        return carry

    lax.fori_loop(1, n, greet, 0)

    load_x.wait()
    load_b.wait()
    load_s.start()

    def coefficients(g, carry):
        c = jnp.dot(basis[g], xext[HALO + g], preferred_element_type=F32).astype(BF16)
        coef[g] = c
        coef_f[g] = c.astype(F32)
        return carry

    lax.fori_loop(0, leaves, coefficients, 0, unroll=leaves)
    load_n.start()

    pl.semaphore_wait(barrier, n - 1)

    def forward_copy(q):
        return pltpu.make_async_remote_copy(
            src_ref=outgoing.at[q],
            dst_ref=received.at[pl.ds(pl.multiple_of(me * rank, rank), rank)],
            send_sem=send1,
            recv_sem=recv1,
            device_id=(q,),
            device_id_type=MESH,
        )

    def peer(step):
        x, z, y, core = me // 32, me // 8 % 4, me // 2 % 4, me % 2
        dx, dz, dy, dc = step
        return (((x + dx) % (n // 32) * 4 + (z + dz) % 4) * 4 + (y + dy) % 4) * 2 + (core + dc) % 2

    to_next = pltpu.make_async_remote_copy(
        src_ref=xext.at[pl.ds(leaves, HALO)],
        dst_ref=xext.at[pl.ds(0, HALO)],
        send_sem=hsend.at[0],
        recv_sem=hrecv.at[0],
        device_id=(lax.rem(me + 1, n),),
        device_id_type=MESH,
    )
    to_prior = pltpu.make_async_remote_copy(
        src_ref=xext.at[pl.ds(HALO, HALO)],
        dst_ref=xext.at[pl.ds(HALO + leaves, HALO)],
        send_sem=hsend.at[1],
        recv_sem=hrecv.at[1],
        device_id=(lax.rem(me + n - 1, n),),
        device_id_type=MESH,
    )
    has_next = me < n - 1
    has_prior = me > 0

    @pl.when(has_next)
    def _():
        to_next.start()

    @pl.when(has_prior)
    def _():
        to_prior.start()

    for step in near_first(n):
        q = peer(step)
        outgoing[q] = coef[target(q)]
        forward_copy(q).start()
    received[pl.ds(pl.multiple_of(me * rank, rank), rank), :] = coef[target(me)]

    @pl.when(jnp.logical_not(has_prior))
    def _():
        xext[0:HALO] = jnp.zeros((HALO, leaf, rhs), BF16)

    @pl.when(jnp.logical_not(has_next))
    def _():
        xext[HALO + leaves :] = jnp.zeros((HALO, leaf, rhs), BF16)

    for pair in range(leaves // 2):
        rows = []
        for g in (2 * pair, 2 * pair + 1):
            for odd in range(2):
                rows.append(coef_f[g, pl.ds(odd, half, stride=2), :])
        tile = jnp.concatenate(rows, axis=0)
        coef_t[:, pair * 2 * rank : (pair + 1) * 2 * rank] = tile.T.astype(BF16)

    keys[...] = jnp.full(keys.shape, -1, jnp.int32)
    for b in range(rows_v.shape[0]):
        keys[b : b + 1, :] = cols_v[b : b + 1, :] * leaves + rows_v[b : b + 1, :]
    b = rows_v.shape[0]
    keys[b : b + 1, 0:nb] = nrows_v[...] + rlast
    keys[b + 1 : b + 2, 0:nb] = ncols_v[...] + klast
    keys[b + 2 : b + 3, 0:n] = send_v[...] + qlast
    chains(keys, prev_v, last_v, parts, id_parts)
    prev_load = pltpu.make_async_copy(prev_v, prev_s, load_sem.at[4])
    last_load = pltpu.make_async_copy(last_v, last_s, load_sem.at[5])
    prev_load.start()
    last_load.start()
    prev_load.wait()
    last_load.wait()

    load_s.wait()

    chained[cb] = jnp.zeros((half, 2 * rank), F32)
    plain[cb] = jnp.zeros((half, 2 * rank), BF16)
    rolled[cb] = jnp.zeros((half, 2 * rank), BF16)

    def spread(t, carry):
        for j in range(half):
            piece = blocks[pl.ds(pl.multiple_of(t * 16, 16), 16), j * 2 * rank : (j + 1) * 2 * rank]
            raw[pl.ds(j, 16, stride=half), :] = piece.astype(F32)
        for s in range(16):
            k = t * 16 + s
            value = raw[s * half : (s + 1) * half, :] + chained[at(prev_s, k)]
            chained[k] = value
            plain[k] = value.astype(BF16)
            rolled[k] = pltpu.roll(value, rank, 1).astype(BF16)
        return carry

    lax.fori_loop(0, cb // 16, spread, 0, unroll=1)

    groups = n // 4
    my_group = me // 4
    part = min(16, n // 2)

    def back_copy(q):
        return pltpu.make_async_remote_copy(
            src_ref=sums.at[q],
            dst_ref=back.at[me],
            send_sem=send2,
            recv_sem=recv2.at[me // part],
            device_id=(q,),
            device_id_type=MESH,
        )

    def mirror(i, carry):
        g = lax.rem(my_group + i * 5, groups)
        rows = []
        for r in range(leaves):
            upper, lower = [], []
            for pair in range(2):
                k0 = last_s[g // 4, g % 4 * 4 * leaves + 2 * pair * leaves + r]
                k1 = last_s[g // 4, g % 4 * 4 * leaves + (2 * pair + 1) * leaves + r]
                upper.append(jnp.where(low_half, plain[k0], rolled[k1]))
                lower.append(jnp.where(low_half, rolled[k0], plain[k1]))
            rows.append(jnp.concatenate(upper, axis=1))
            rows.append(jnp.concatenate(lower, axis=1))
        tile = jnp.concatenate(rows, axis=0)
        dense[g] = tile
        product = jnp.dot(coef_t[...], tile, preferred_element_type=F32)
        for pair in range(2):
            part = product[:, pair * 2 * rank : (pair + 1) * 2 * rank]
            top, bottom = part[:rank], part[rank:]
            turned = pltpu.roll(jnp.where(low, bottom, top), rank, 1)
            sums[g * 4 + 2 * pair] = jnp.where(low, top, turned).astype(BF16)
            sums[g * 4 + 2 * pair + 1] = jnp.where(low, turned, bottom).astype(BF16)
        for s in range(4):
            q = g * 4 + s

            @pl.when(q != me)
            def _():
                back_copy(q).start()

            @pl.when(q == me)
            def _():
                back[me] = sums[me]

        return carry

    lax.fori_loop(0, groups, mirror, 0, unroll=2)

    for g in range(leaves):
        x_t[g] = xext[HALO + g].astype(F32).T.astype(BF16)
        basis_t[g] = basis[g].astype(F32).T.astype(BF16)

    @pl.when(has_prior)
    def _():
        to_next.wait_recv()

    @pl.when(has_next)
    def _():
        to_prior.wait_recv()

    load_n.wait()
    work[nb] = jnp.zeros((leaf, rhs), F32)

    def near_rows(k, carry):
        y = jnp.dot(near[k], xext[ncols_ref[k]], preferred_element_type=F32)
        work[k] = y + work[at(prev_s, rprev + k)]
        return carry

    lax.fori_loop(0, nb, near_rows, 0, unroll=8)
    for g in range(leaves):
        near_sum[g] = work[at(last_s, rlast + g)]

    def near_cols(k, carry):
        y = jnp.dot(x_t[nrows_ref[k]], near[k], preferred_element_type=F32)
        before = work[at(prev_s, kprev + k)]
        for h in range(2):
            rows = slice(h * rhs, (h + 1) * rhs)
            work[k, rows, :] = y[:, rows] + before[rows]
        return carry

    lax.fori_loop(0, nb, near_cols, 0, unroll=8)

    def spread_of(c):
        return work[at(last_s, klast + c)]

    for h in range(HALO):
        rim_out[0, h] = spread_of(h).astype(BF16)
        rim_out[1, h] = spread_of(HALO + leaves + h).astype(BF16)
    rim_prior = pltpu.make_async_remote_copy(
        src_ref=rim_out.at[0],
        dst_ref=rim_in.at[0],
        send_sem=rsend.at[0],
        recv_sem=rrecv.at[0],
        device_id=(lax.rem(me + n - 1, n),),
        device_id_type=MESH,
    )
    rim_next = pltpu.make_async_remote_copy(
        src_ref=rim_out.at[1],
        dst_ref=rim_in.at[1],
        send_sem=rsend.at[1],
        recv_sem=rrecv.at[1],
        device_id=(lax.rem(me + 1, n),),
        device_id_type=MESH,
    )

    @pl.when(has_prior)
    def _():
        rim_prior.start()

    @pl.when(has_next)
    def _():
        rim_next.start()

    def add_turned(g, y):
        for h in range(2):
            rows = slice(h * rhs, (h + 1) * rhs)
            near_sum[g, rows, :] += y[rows].T

    for g in range(leaves):
        add_turned(g, spread_of(HALO + g))

    others = pl.ds(0, (n - 1) * rank)
    all_forward = pltpu.make_async_remote_copy(
        src_ref=received.at[others],
        dst_ref=received.at[others],
        send_sem=send1,
        recv_sem=recv1,
        device_id=(lax.rem(me + 1, n),),
        device_id_type=MESH,
    )
    all_forward.wait_recv()
    all_forward.wait_send()
    total[...] = jnp.zeros_like(total)
    step = min(4, groups)

    def forward(i, carry):
        acc = total[...]
        for s in range(step):
            g = i * step + s
            c = received[pl.ds(pl.multiple_of(g * 4 * rank, 4 * rank), 4 * rank), :]
            acc = acc + jnp.dot(dense[g], c, preferred_element_type=F32)
        total[...] = acc
        return carry

    lax.fori_loop(0, groups // step, forward, 0)

    @pl.when(has_next)
    def _():
        rim_prior.wait_recv()
        for h in range(HALO):
            add_turned(leaves - HALO + h, rim_in[0, h].astype(F32))

    @pl.when(has_prior)
    def _():
        rim_next.wait_recv()
        for h in range(HALO):
            add_turned(h, rim_in[1, h].astype(F32))

    back_sum[n] = jnp.zeros((rank, rhs), F32)

    def arrived(i, count):
        return pltpu.make_async_remote_copy(
            src_ref=back.at[pl.ds(0, count)],
            dst_ref=back.at[pl.ds(0, count)],
            send_sem=send2,
            recv_sem=recv2.at[i],
            device_id=(lax.rem(me + 1, n),),
            device_id_type=MESH,
        )

    def returned(i, carry):
        @pl.when(me // part == i)
        def _():
            arrived(i, part - 1).wait_recv()

        @pl.when(me // part != i)
        def _():
            arrived(i, part).wait_recv()

        for s in range(part):
            q = i * part + s
            back_sum[q] = back[q].astype(F32) + back_sum[at(prev_s, qprev + q)]
        return carry

    lax.fori_loop(0, n // part, returned, 0)
    arrived(0, n - 1).wait_send()

    def store(g):
        return pltpu.make_async_copy(out.at[g], out_hbm.at[g], load_sem.at[6 + g])

    for g in range(leaves):
        y = back_sum[at(last_s, qlast + g)]
        turned = jnp.concatenate([y, pltpu.roll(y, rank, 1)], axis=0).T
        far_f[g, pl.ds(0, half, stride=2), :] = total[g * rank : g * rank + half, :]
        far_f[g, pl.ds(1, half, stride=2), :] = total[g * rank + half : (g + 1) * rank, :]
        far = (far_f[g] + turned[:rank]).astype(BF16)
        down = jnp.dot(basis_t[g], far, preferred_element_type=F32)
        out[g] = (down + near_sum[g]).astype(BF16)
        store(g).start()

    @pl.when(has_next)
    def _():
        to_next.wait_send()
        rim_next.wait_send()

    @pl.when(has_prior)
    def _():
        to_prior.wait_send()
        rim_prior.wait_send()

    for g in range(leaves):
        store(g).wait()


def per_device(
    features,
    basis_t,
    send_list,
    couple_rows,
    couple_cols,
    couple_blocks,
    near_rows,
    near_cols,
    near_blocks,
):
    n = lax.axis_size("clus")
    leaves, rank, leaf = basis_t.shape
    rhs = features.shape[1]
    cb, nb = couple_blocks.shape[0], near_blocks.shape[0]
    send = send_list.reshape(-1)
    base = -(-n * leaves // 128) * 128
    key_rows = cb // 128 + 3
    half = rank // 2
    wide = leaves + 2 * HALO
    dma = pltpu.SemaphoreType.DMA
    smem = pl.BlockSpec(memory_space=pltpu.SMEM)
    anywhere = pl.BlockSpec(memory_space=pl.ANY)
    return pl.pallas_call(
        functools.partial(kernel, n, leaves, rank, leaf, rhs, cb, nb),
        out_shape=jax.ShapeDtypeStruct((leaves, leaf, rhs), BF16),
        in_specs=[smem] * 3 + [pl.BlockSpec(memory_space=pltpu.VMEM)] * 5 + [anywhere] * 4,
        out_specs=anywhere,
        scratch_shapes=[
            pltpu.VMEM((wide, leaf, rhs), BF16),
            pltpu.VMEM((leaves, rank, leaf), BF16),
            pltpu.VMEM((leaves, leaf, rank), BF16),
            pltpu.VMEM(couple_blocks.shape, BF16),
            pltpu.VMEM(near_blocks.shape, BF16),
            pltpu.VMEM((leaves, rank, rhs), BF16),
            pltpu.VMEM((leaves, rank, rhs), F32),
            pltpu.VMEM((rhs, leaves * rank), BF16),
            pltpu.VMEM((leaves, rhs, leaf), BF16),
            pltpu.VMEM((n, rank, rhs), BF16),
            pltpu.VMEM((n * rank, rhs), BF16),
            pltpu.VMEM((cb + 1, half, 2 * rank), BF16),
            pltpu.VMEM((cb + 1, half, 2 * rank), BF16),
            pltpu.VMEM((n // 4, leaves * rank, 4 * rank), BF16),
            pltpu.VMEM((n, rank, rhs), BF16),
            pltpu.VMEM((n, rank, rhs), BF16),
            pltpu.VMEM((leaves * rank, rhs), F32),
            pltpu.VMEM((16 * half, 2 * rank), F32),
            pltpu.VMEM((cb + 1, half, 2 * rank), F32),
            pltpu.VMEM((nb + 1, leaf, rhs), F32),
            pltpu.VMEM((n + 1, rank, rhs), F32),
            pltpu.VMEM((leaves, leaf, rhs), F32),
            pltpu.VMEM((2, HALO, leaf, rhs), BF16),
            pltpu.VMEM((2, HALO, leaf, rhs), BF16),
            pltpu.VMEM((leaves, leaf, rhs), BF16),
            pltpu.VMEM((leaves, rank, rhs), F32),
            pltpu.VMEM((key_rows, 128), jnp.int32),
            pltpu.VMEM((key_rows, 128), jnp.int32),
            pltpu.VMEM((base // 128 + 1, 128), jnp.int32),
            pltpu.SMEM((key_rows, 128), jnp.int32),
            pltpu.SMEM((base // 128 + 1, 128), jnp.int32),
            dma((6 + leaves,)),
            dma,
            dma,
            dma,
            dma((n // min(16, n // 2),)),
            dma((2,)),
            dma((2,)),
            dma((2,)),
            dma((2,)),
        ],
        compiler_params=pltpu.CompilerParams(
            collective_id=0, has_side_effects=True, vmem_limit_bytes=60 * 1024 * 1024
        ),
    )(
        send,
        near_rows,
        near_cols,
        couple_rows.reshape(-1, 128),
        couple_cols.reshape(-1, 128),
        near_rows.reshape(1, nb),
        near_cols.reshape(1, nb),
        send.reshape(1, n),
        features.reshape(leaves, leaf, rhs),
        basis_t,
        couple_blocks,
        near_blocks,
    ).reshape(features.shape)


def solution(mesh):
    placed = (
        P("clus", None),
        P("clus", None, None),
        P("clus", None, None),
        P("clus"),
        P("clus"),
        P("clus", None),
        P("clus"),
        P("clus"),
        P("clus", None, None),
    )
    return jax.shard_map(
        per_device, mesh=mesh, in_specs=placed, out_specs=P("clus", None), check_vma=False
    )
```
